32 devices in a mesh: ta: 4 (over y, core), gz: 4 (over z), xy: 2 (over x).
Axes of the slice: x: 2, y: 2, z: 4, core: 2. Of those that a mesh axis runs over, the one named last changes fastest.
Arguments:
- right_side: float32 [2, 3, 16, 16, 8, 16], P(None, None, 'ta', 'gz', 'xy'), may hold values from -6 to 6
- links: bfloat16 [3, 3, 16, 16, 8, 256], P(None, None, 'ta', 'gz', 'xy'), may hold values from -0.59765625 to 0.59765625
- block_inverse: bfloat16 [48, 8, 8, 4, 768], P(None, 'ta', 'gz', 'xy')
- near_fine: bfloat16 [24, 8, 8, 4, 768], P(None, 'ta', 'gz', 'xy'), may hold values from -0.875 to 0.875
- mid_stencil: bfloat16 [9, 24, 8, 8, 4, 384], P(None, None, 'ta', 'gz', 'xy')
- mid_jacobi: bfloat16 [24, 8, 8, 4, 384], P(None, 'ta', 'gz', 'xy')
- near_mid: bfloat16 [48, 4, 4, 2, 3072], P(None, 'ta', 'gz', 'xy'), may hold values from -0.3125 to 0.3125
- coarse_stencil: bfloat16 [9, 2, 4, 4, 2, 192, 48], P(None, None, 'ta', 'gz', 'xy')
- coarse_jacobi: bfloat16 [2, 4, 4, 2, 192, 48], P(None, 'ta', 'gz', 'xy')
Outputs:
- solution: float32 [2, 3, 16, 16, 8, 16], P(None, None, 'ta', 'gz', 'xy')
- residual: float32 [2, 3, 16, 16, 8, 16], P(None, None, 'ta', 'gz', 'xy')
The draws below stay inside these ranges and needn't reach their ends.
All inputs are finite; a program needn't handle non-finite values.
Results may differ from the reference program's by a relative error of at most 0.0003.
Values may be sent and summed in bfloat16 or wider, within the bound.
No kernel may reach another device: no remote copies, remote signals or barrier semaphores. Data moves between devices by JAX's collectives and lax.ppermute only.
A program may use at most 256 MiB of HBM per device.

```python
import math
import jax
import jax.numpy as jnp
from jax import lax

NV1 = 24
NV2 = 48
SWEEPS = 4
CYCLES = 2
NT = 16
NZ = 16
NX = 8
NY = 16


def diag_heavy(key, order_n, site_dims, scale_low, scale_high, noise_level):
    key_noise, key_scale = jax.random.split(key)
    rough = jax.random.normal(key_noise, (2, order_n, order_n) + site_dims, jnp.float32) * (noise_level / math.sqrt(order_n))
    scales = jnp.exp(jax.random.uniform(key_scale, (order_n,) + site_dims, jnp.float32, math.log(scale_low), math.log(scale_high)))
    identity = jnp.eye(order_n, dtype=jnp.float32).reshape((order_n, order_n) + (1,) * len(site_dims))
    return jnp.stack([rough[0] + identity * scales[:, None], rough[1]])


def stencil_draw(key, order_n, site_dims):
    key_self, key_hops = jax.random.split(key)
    self_term = diag_heavy(key_self, order_n, site_dims, 0.8, 1.6, 0.3)
    hop_terms = jax.random.normal(key_hops, (8, 2, order_n, order_n) + site_dims, jnp.float32) * (0.2 / math.sqrt(order_n))
    return jnp.concatenate([self_term[None], hop_terms], axis=0)


def pack_matrix(matrix):
    a, o, i, t, z, x, y = matrix.shape
    return matrix.transpose(1, 3, 4, 5, 0, 2, 6).reshape(o, t, z, x, a * i * y)


def pack_stencil(stencil):
    k, a, o, i, t, z, x, y = stencil.shape
    return stencil.transpose(0, 2, 4, 5, 6, 1, 3, 7).reshape(k, o, t, z, x, a * i * y)


def draw_block_inverse(key, part):
    key = jax.random.fold_in(key, 11)
    return pack_matrix(diag_heavy(key, 48, (NT // 2, NZ // 2, NX // 2, NY // 2), 0.6, 1.2, 0.25)).astype(jnp.bfloat16)


def draw_mid_stencil(key, part):
    key = jax.random.fold_in(key, 12)
    return pack_stencil(stencil_draw(key, NV1, (NT // 2, NZ // 2, NX // 2, NY // 2))).astype(jnp.bfloat16)


def draw_mid_jacobi(key, part):
    key = jax.random.fold_in(key, 13)
    return pack_matrix(diag_heavy(key, NV1, (NT // 2, NZ // 2, NX // 2, NY // 2), 0.4, 0.8, 0.15)).astype(jnp.bfloat16)


def draw_coarse_stencil(key, part):
    key = jax.random.fold_in(key, 14)
    drawn = stencil_draw(key, NV2, (NT // 4, NZ // 4, NX // 4, NY // 4))
    moved = drawn.transpose(0, 1, 4, 5, 6, 7, 2, 3)
    return moved.reshape(9, 2, NT // 4, NZ // 4, NX // 4, NY // 4 * NV2, NV2).astype(jnp.bfloat16)


def draw_coarse_jacobi(key, part):
    key = jax.random.fold_in(key, 15)
    drawn = diag_heavy(key, NV2, (NT // 4, NZ // 4, NX // 4, NY // 4), 0.4, 0.8, 0.15)
    moved = drawn.transpose(0, 3, 4, 5, 6, 1, 2)
    return moved.reshape(2, NT // 4, NZ // 4, NX // 4, NY // 4 * NV2, NV2).astype(jnp.bfloat16)


def levels(own_key, shape, pieces, low, high):
    def one(position, blocks):
        draws = jax.random.uniform(jax.random.fold_in(jax.random.fold_in(own_key, 6), position), (blocks,), jnp.float32, low / len(pieces), high / len(pieces))
        return jnp.repeat(jnp.exp(draws), shape[position] // blocks).reshape((-1,) + (1,) * (len(shape) - position - 1))

    factor_of = one(*pieces[0])
    for cut in pieces[1:]:
        factor_of = factor_of * one(*cut)
    return factor_of


def bell_draw(rng, dims, scale, limit, cuts=(), held_as=jnp.bfloat16):
    result = jax.random.normal(rng, dims, jnp.float32) * scale
    if len(cuts) > 0:
        result = levels(rng, dims, cuts, -0.22, 0.18) * result
    return jnp.clip(result, min=-limit, max=limit).astype(held_as)


def setup_inputs(seed: int = 0) -> dict:
    streams_of = jax.random.split(jax.random.key(seed), 10)
    right_side = bell_draw(streams_of[0], (2, 3, NT, NZ, NX, NY), 1.0, 6.0, ((2, 4), (3, 4), (4, 2)), jnp.float32)
    links = bell_draw(streams_of[1], (3, 3, NT, NZ, NX, 16 * NY), 0.08, 0.59765625, ((2, 4), (3, 4), (4, 2)))
    block_inverse = draw_block_inverse(jax.random.fold_in(streams_of[9], 71), 0)
    near_fine = bell_draw(streams_of[3], (NV1, NT // 2, NZ // 2, NX // 2, 96 * (NY // 2)), 48 ** -0.5, 0.875, ((1, 4), (2, 4), (3, 2)))
    mid_stencil = draw_mid_stencil(jax.random.fold_in(streams_of[9], 71), 0)
    mid_jacobi = draw_mid_jacobi(jax.random.fold_in(streams_of[9], 71), 0)
    near_mid = bell_draw(streams_of[6], (NV2, NT // 4, NZ // 4, NX // 4, 32 * NV1 * (NY // 4)), (16 * NV1) ** -0.5, 0.3125, ((1, 4), (2, 4), (3, 2)))
    coarse_stencil = draw_coarse_stencil(jax.random.fold_in(streams_of[9], 71), 0)
    coarse_jacobi = draw_coarse_jacobi(jax.random.fold_in(streams_of[9], 71), 0)
    return dict(right_side=right_side, links=links, block_inverse=block_inverse, near_fine=near_fine, mid_stencil=mid_stencil, mid_jacobi=mid_jacobi, near_mid=near_mid, coarse_stencil=coarse_stencil, coarse_jacobi=coarse_jacobi)


MASS = 1.0
PRECISE = lax.Precision.HIGHEST


def unpack_links(packed):
    rows, cols, t, z, x, last = packed.shape
    y = last // 16
    shaped = packed.reshape(rows, cols, t, z, x, 4, 2, 2, y)
    return shaped.transpose(6, 5, 7, 0, 1, 2, 3, 4, 8)


def unpack_matrix(packed, inner):
    outer, t, z, x, last = packed.shape
    y = last // (2 * inner)
    shaped = packed.reshape(outer, t, z, x, 2, inner, y)
    return shaped.transpose(4, 0, 5, 1, 2, 3, 6)


def unpack_stencil(packed):
    terms, outer, t, z, x, last = packed.shape
    y = last // (2 * outer)
    shaped = packed.reshape(terms, outer, t, z, x, 2, outer, y)
    return shaped.transpose(0, 5, 1, 6, 2, 3, 4, 7)


def unpack_coarse_stencil(packed):
    terms, parts, t, z, x, merged, inner = packed.shape
    y = merged // inner
    shaped = packed.reshape(terms, parts, t, z, x, y, inner, inner)
    return shaped.transpose(0, 1, 6, 7, 2, 3, 4, 5)


def unpack_coarse_jacobi(packed):
    parts, t, z, x, merged, inner = packed.shape
    y = merged // inner
    shaped = packed.reshape(parts, t, z, x, y, inner, inner)
    return shaped.transpose(0, 5, 6, 1, 2, 3, 4)


def contract(left, right):
    return jnp.einsum('oi...,i...->o...', left, right, precision=PRECISE)


def contract_back(left, right):
    return jnp.einsum('oi...,o...->i...', left, right, precision=PRECISE)


def product(matrix_re, matrix_im, vector):
    return jnp.stack([contract(matrix_re, vector[0]) - contract(matrix_im, vector[1]),
                      contract(matrix_re, vector[1]) + contract(matrix_im, vector[0])])


def transposed(matrix_re, matrix_im, vector):
    return jnp.stack([contract_back(matrix_re, vector[0]) - contract_back(matrix_im, vector[1]),
                      contract_back(matrix_re, vector[1]) + contract_back(matrix_im, vector[0])])


def to_blocks(field):
    a, c, t, z, x, y = field.shape
    folded = field.reshape(a, c, t // 2, 2, z // 2, 2, x // 2, 2, y // 2, 2)
    folded = folded.transpose(0, 1, 3, 5, 7, 9, 2, 4, 6, 8)
    return folded.reshape(a, c * 16, t // 2, z // 2, x // 2, y // 2)


def from_blocks(blocked, colours):
    a, d, t, z, x, y = blocked.shape
    folded = blocked.reshape(a, colours, 2, 2, 2, 2, t, z, x, y)
    folded = folded.transpose(0, 1, 6, 2, 7, 3, 8, 4, 9, 5)
    return folded.reshape(a, colours, 2 * t, 2 * z, 2 * x, 2 * y)


def phases(lattice_dims):
    coord_t = lax.broadcasted_iota(jnp.int32, lattice_dims, 0)
    coord_z = lax.broadcasted_iota(jnp.int32, lattice_dims, 1)
    coord_x = lax.broadcasted_iota(jnp.int32, lattice_dims, 2)
    ones = jnp.ones(lattice_dims, jnp.float32)
    return [ones,
            (1 - 2 * (coord_t % 2)).astype(jnp.float32),
            (1 - 2 * ((coord_t + coord_z) % 2)).astype(jnp.float32),
            (1 - 2 * ((coord_t + coord_z + coord_x) % 2)).astype(jnp.float32)]


def fine_apply(field, link_values, phase_sign):
    summed = MASS * field
    for direction in range(4):
        axis_pos = 2 + direction
        hopping = 0.0
        for link_kind, reach in ((0, 1), (1, 3)):
            matrix = link_values[link_kind, direction]
            forward = product(matrix[0], matrix[1], jnp.roll(field, -reach, axis_pos))
            backward = jnp.roll(transposed(matrix[0], -matrix[1], field), reach, axis_pos)
            hopping = hopping + forward - backward
        summed = summed + 0.5 * phase_sign[direction] * hopping
    return summed


def stencil_apply(stencil, vector):
    self_term = stencil[0].astype(jnp.float32)
    summed = product(self_term[0], self_term[1], vector)
    for direction in range(4):
        for offset, stencil_k in ((1, 2 * direction + 1), (-1, 2 * direction + 2)):
            hop_term = stencil[stencil_k].astype(jnp.float32)
            summed = summed + product(hop_term[0], hop_term[1], jnp.roll(vector, -offset, 2 + direction))
    return summed


def jacobi_sweeps(jacobi, source, apply_fn):
    solved = product(jacobi[0], jacobi[1], source)
    for sweep in range(SWEEPS):
        solved = solved + product(jacobi[0], jacobi[1], source - apply_fn(solved))
    return solved


def reference(right_side, links, block_inverse, near_fine, mid_stencil, mid_jacobi, near_mid, coarse_stencil, coarse_jacobi):
    link_values = unpack_links(links).astype(jnp.float32)
    phase_sign = phases(right_side.shape[2:])
    block_matrix = unpack_matrix(block_inverse, 48).astype(jnp.float32)
    near_one = unpack_matrix(near_fine, 48).astype(jnp.float32)
    near_two = unpack_matrix(near_mid, near_mid.shape[4] * 4 // (2 * right_side.shape[5])).astype(jnp.float32)
    mid_smooth = unpack_matrix(mid_jacobi, mid_jacobi.shape[0]).astype(jnp.float32)
    mid_terms = unpack_stencil(mid_stencil)
    coarse_terms = unpack_coarse_stencil(coarse_stencil)
    coarse_smooth = unpack_coarse_jacobi(coarse_jacobi).astype(jnp.float32)
    solution = jnp.zeros_like(right_side)
    residual = right_side
    for cycle_no in range(CYCLES):
        solution = solution + from_blocks(product(block_matrix[0], block_matrix[1], to_blocks(residual)), 3)
        residual = right_side - fine_apply(solution, link_values, phase_sign)
        mid_res = product(near_one[0], -near_one[1], to_blocks(residual))
        mid_sol = product(mid_smooth[0], mid_smooth[1], mid_res)
        coarse_res = product(near_two[0], -near_two[1], to_blocks(mid_res - stencil_apply(mid_terms, mid_sol)))
        coarse_sol = jacobi_sweeps(coarse_smooth, coarse_res, lambda vector: stencil_apply(coarse_terms, vector))
        mid_sol = mid_sol + from_blocks(transposed(near_two[0], near_two[1], coarse_sol), mid_res.shape[1])
        mid_sol = mid_sol + product(mid_smooth[0], mid_smooth[1], mid_res - stencil_apply(mid_terms, mid_sol))
        solution = solution + from_blocks(transposed(near_one[0], near_one[1], mid_sol), 3)
        residual = right_side - fine_apply(solution, link_values, phase_sign)
        solution = solution + from_blocks(product(block_matrix[0], block_matrix[1], to_blocks(residual)), 3)
        residual = right_side - fine_apply(solution, link_values, phase_sign)
    return solution, residual
```

```python
import jax
import jax.numpy as jnp
from jax import lax
from jax.sharding import PartitionSpec as P
import jax.experimental.pallas as pl
from jax.experimental.pallas import tpu as pltpu

SWEEPS = 4
CYCLES = 2
F32 = jnp.float32
BF16 = jnp.bfloat16
HIGHEST = lax.Precision.HIGHEST
LANE_BITS = (64, 32, 16)
ROW_BITS = (4, 2, 1)
VMEM_BYTES = 24 << 20


class Site:
    def __init__(self):
        self.lane = lax.broadcasted_iota(jnp.int32, (8, 128), 1)
        self.row = lax.broadcasted_iota(jnp.int32, (8, 128), 0)
        self.by = self.lane & 7

    def lane_bit(self, d):
        return (self.lane & d) != 0

    def row_bit(self, d):
        return (self.row & d) != 0

    def first(self, direction):
        return ((self.lane & LANE_BITS[direction]) | (self.row & ROW_BITS[direction])) == 0

    def last(self, direction):
        return self.lane_bit(LANE_BITS[direction]) & self.row_bit(ROW_BITS[direction])


def left(x, s):
    s = s % 128
    return pltpu.roll(x, (128 - s) % 128, 1) if s else x


def up(x, s):
    s = s % 8
    return pltpu.roll(x, (8 - s) % 8, 0) if s else x


def flip_lane(site, x, d):
    if d == 64:
        return left(x, 64)
    return jnp.where(site.lane_bit(d), left(x, -d), left(x, d))


def flip_row(site, x, d):
    if d == 4:
        return up(x, 4)
    return jnp.where(site.row_bit(d), up(x, -d), up(x, d))


def cyclic(site, x, direction, sign):
    d = LANE_BITS[direction]
    flipped = flip_lane(site, x, d)
    both = flip_row(site, flipped, ROW_BITS[direction])
    if sign > 0:
        return jnp.where(site.lane_bit(d), both, flipped)
    return jnp.where(site.lane_bit(d), flipped, both)


def by_roll(site, x, base, q):
    moved = left(x, base + q)
    if q == 0:
        return moved
    if q > 0:
        return jnp.where(site.by >= 8 - q, left(x, base + q - 8), moved)
    return jnp.where(site.by < -q, left(x, base + q + 8), moved)


def shift_y(site, x, n):
    found = []
    for c in (0, 1):
        c_new = (c + n) % 2
        q = (c + n - c_new) // 2
        found.append(by_roll(site, x, 8 * (c_new - c), q))
    return jnp.where(site.lane_bit(8), found[1], found[0])


def link(links_ref, mu, kind, part, r, c):
    return links_ref[((mu * 2 + kind) * 2 + part) * 9 + r * 3 + c]


def link_apply(links_ref, mu, kind, field):
    out = [None] * 6
    for r in range(3):
        re = im = None
        for c in range(3):
            g_re = link(links_ref, mu, kind, 0, r, c)
            g_im = link(links_ref, mu, kind, 1, r, c)
            a = g_re * field[c] - g_im * field[3 + c]
            b = g_re * field[3 + c] + g_im * field[c]
            re = a if re is None else re + a
            im = b if im is None else im + b
        out[r] = re
        out[3 + r] = im
    return out


def link_adjoint(links_ref, mu, kind, field):
    out = [None] * 6
    for c in range(3):
        re = im = None
        for r in range(3):
            g_re = link(links_ref, mu, kind, 0, r, c)
            g_im = link(links_ref, mu, kind, 1, r, c)
            a = g_re * field[r] + g_im * field[3 + r]
            b = g_re * field[3 + r] - g_im * field[r]
            re = a if re is None else re + a
            im = b if im is None else im + b
        out[c] = re
        out[3 + c] = im
    return out


def add(xs, ys):
    return [x + y for x, y in zip(xs, ys)]


def sub(xs, ys):
    return [x - y for x, y in zip(xs, ys)]


def fine_send(site, links_ref, field, acc_ref, sent_refs):
    acc = list(field)
    for kind, reach in ((0, 1), (1, 3)):
        acc = add(acc, link_apply(links_ref, 3, kind, [shift_y(site, x, reach) for x in field]))
        back = link_adjoint(links_ref, 3, kind, field)
        acc = sub(acc, [shift_y(site, x, -reach) for x in back])
    for direction in range(3):
        near = [cyclic(site, x, direction, -1) for x in link_adjoint(links_ref, direction, 0, field)]
        far = link_adjoint(links_ref, direction, 1, field)
        first, last = site.first(direction), site.last(direction)
        ref, base = sent_refs[direction]
        for i in range(6):
            ref[base + i] = jnp.where(first, near[i], far[i])
        acc = [
            a - jnp.where(first, 0.0, n) - jnp.where(last, cyclic(site, f, direction, 1), 0.0)
            for a, n, f in zip(acc, near, far)
        ]
    for i in range(6):
        acc_ref[i] = acc[i]


def fine_receive(site, links_ref, field, acc, ahead, behind):
    out = acc
    for direction in range(3):
        first, last = site.first(direction), site.last(direction)
        nxt = ahead[direction]
        one = [cyclic(site, jnp.where(first, n, x), direction, 1) for n, x in zip(nxt, field)]
        out = add(out, link_apply(links_ref, direction, 0, one))
        three = [cyclic(site, jnp.where(last, x, n), direction, -1) for n, x in zip(nxt, field)]
        out = add(out, link_apply(links_ref, direction, 1, three))
        out = [
            o - jnp.where(first, b, 0.0) - jnp.where(last, 0.0, cyclic(site, b, direction, 1))
            for o, b in zip(out, behind[direction])
        ]
    return out


def merge(site, d, a, b):
    bit = site.lane_bit(d)
    return jnp.where(bit, b, a) + left(jnp.where(bit, a, b), d)


def tree(site, leaf, base, n):
    if n == 2:
        a, b = leaf(base)
    else:
        a = tree(site, leaf, base, n // 2)
        b = tree(site, leaf, base + n // 2, n // 2)
    return [merge(site, 4 * n, x, y) for x, y in zip(a, b)]


def two_rows(ref, o):
    return ref[pl.ds(o * 8, 16), :].astype(F32)


def dot_tiles(block, row, x):
    total = None
    for j, v in enumerate(x):
        term = block[row : row + 8, 128 * j : 128 * j + 128] * v
        total = term if total is None else total + term
    return total


def pair_leaf(terms):
    def leaf(o):
        sums = [[None, None], [None, None]]
        for ref, base, x_re, x_im in terms:
            block = two_rows(ref, base + o)
            for h in range(2):
                for p, x in enumerate((x_re, x_im)):
                    t = dot_tiles(block, 8 * h, x)
                    sums[h][p] = t if sums[h][p] is None else sums[h][p] + t
        return sums

    return leaf


def fine_matrix(site, ref, field):
    x_re = field[:3] + [-x for x in field[3:]]
    x_im = field[3:] + field[:3]
    out = [tree(site, pair_leaf([(ref, 0, x_re, x_im)]), 16 * c, 16) for c in range(3)]
    return [o[0] for o in out] + [o[1] for o in out]


def mid_gather(site, terms):
    leaf = pair_leaf(terms)
    eight = [tree(site, leaf, 8 * j, 8) for j in range(3)]
    return [
        merge(site, 64, eight[0][0], eight[1][0]),
        merge(site, 64, eight[2][0], eight[0][1]),
        merge(site, 64, eight[1][1], eight[2][1]),
    ]


def swap_parts(site, v):
    low = jnp.logical_not(site.lane_bit(64))
    r = [left(x, 64) for x in v]
    return [jnp.where(low, r[1], r[2]), jnp.where(low, r[2], r[0]), jnp.where(low, r[0], r[1])]


def im_negated(site, v):
    return [v[0], jnp.where(site.lane_bit(64), -v[1], v[1]), -v[2]]


def mid_x(site, v):
    return im_negated(site, v), swap_parts(site, v)


def mid_x_conj(site, v):
    return v, im_negated(site, swap_parts(site, v))


def restrict_fine(site, near_ref, field):
    x_im = field[3:] + [-x for x in field[:3]]
    return mid_gather(site, [(near_ref, 0, field, x_im)])


def mid_matrix(site, ref, v):
    x_re, x_im = mid_x(site, v)
    return mid_gather(site, [(ref, 0, x_re, x_im)])


def mid_stencil_apply(site, ref, v, ahead, behind):
    shifted = [v]
    for direction in range(3):
        d = ROW_BITS[direction]
        bit = site.row_bit(d)
        shifted.append([flip_row(site, jnp.where(bit, x, n), d) for x, n in zip(v, ahead[direction])])
        shifted.append([flip_row(site, jnp.where(bit, n, x), d) for x, n in zip(v, behind[direction])])
    shifted.append([by_roll(site, x, 0, 1) for x in v])
    shifted.append([by_roll(site, x, 0, -1) for x in v])
    return mid_gather(site, [(ref, 24 * k) + mid_x(site, s) for k, s in enumerate(shifted)])


def spread(site, v, ref):
    def down(x, base, d):
        if d == 4:
            ref[base] = x
            return
        bit = site.lane_bit(d)
        r = left(x, d)
        down(jnp.where(bit, r, x), base, d // 2)
        down(jnp.where(bit, x, r), base + d // 8, d // 2)

    for j, x in enumerate(v):
        down(x, 16 * j, 64)


def prolong_fine(site, near_ref, v, spread_ref):
    spread(site, v, spread_ref)
    a, b = [0.0] * 6, [0.0] * 6
    for o in range(0, 24, 2):
        block = two_rows(near_ref, o)
        for h in range(2):
            y_re, y_im = spread_ref[o + h], spread_ref[24 + o + h]
            for j in range(6):
                n = block[8 * h : 8 * h + 8, 128 * j : 128 * j + 128]
                a[j] = a[j] + n * y_re
                b[j] = b[j] + n * y_im
    return [a[j] - b[3 + j] for j in range(3)] + [a[3 + j] + b[j] for j in range(3)]


def iota2(shape, axis):
    return lax.broadcasted_iota(jnp.int32, shape, axis)


def pick_y(part):
    row, lane = iota2((8, 128), 0), iota2((8, 128), 1)
    return (row == part * 4 + ((lane & 7) >> 1)).astype(F32)


def restrict_mid(site, near_ref, v, tile_ref):
    x_re, x_im = mid_x_conj(site, v)
    for o in range(0, 48, 2):
        block = two_rows(near_ref, o)
        for h in range(2):
            tile_ref[0, pl.ds(8 * (o + h), 8), :] = dot_tiles(block, 8 * h, x_re)
            tile_ref[1, pl.ds(8 * (o + h), 8), :] = dot_tiles(block, 8 * h, x_im)
    dims = (((1,), (1,)), ((), ()))
    z = None
    for p in range(2):
        t = lax.dot_general(pick_y(p), tile_ref[p], dims, precision=HIGHEST, preferred_element_type=F32)
        z = t if z is None else z + t
    select = ((iota2((384, 48), 0) >> 3) == iota2((384, 48), 1)).astype(F32)
    return jnp.dot(z, select, precision=HIGHEST, preferred_element_type=F32)


def prolong_mid(site, near_ref, y3, row_ref):
    dims = (((0,), (0,)), ((), ()))
    for p in range(2):
        row_ref[p] = lax.dot_general(y3, pick_y(p), dims, precision=HIGHEST, preferred_element_type=F32)
    a, b = [0.0] * 3, [0.0] * 3
    for o in range(0, 48, 2):
        block = two_rows(near_ref, o)
        for h in range(2):
            y_re = jnp.broadcast_to(row_ref[0, pl.ds(o + h, 1), :], (8, 128))
            y_im = jnp.broadcast_to(row_ref[1, pl.ds(o + h, 1), :], (8, 128))
            for j in range(3):
                n = block[8 * h : 8 * h + 8, 128 * j : 128 * j + 128]
                a[j] = a[j] + n * y_re
                b[j] = b[j] + n * y_im
    return add(a, swap_parts(site, [-x for x in im_negated_keep(site, b)]))


def im_negated_keep(site, v):
    return [-v[0], jnp.where(site.lane_bit(64), v[1], -v[1]), v[2]]


def coarse_rows(v):
    high = v.astype(BF16).astype(F32)
    return jnp.concatenate([high, v - high], axis=0).astype(BF16)


def coarse_matrix(terms):
    row = iota2((8, 48), 0)
    total = None
    for ref, base, v in terms:
        turned = jnp.where(row < 4, -up(v, 4), up(v, 4))
        for a, x in enumerate((v, turned)):
            t = jnp.dot(coarse_rows(x), ref[pl.ds(base + 48 * a, 48), :], preferred_element_type=F32)
            total = t if total is None else total + t
    both = total[:8] + total[8:]
    out = None
    for y in range(4):
        t = jnp.where((row & 3) == y, both[:, 48 * y : 48 * y + 48], 0.0)
        out = t if out is None else out + t
    return out


def coarse_stencil_apply(ref, v, ahead, behind):
    y = iota2((8, 48), 0) & 3
    shifted = [v]
    for direction in range(3):
        shifted += [ahead[direction], behind[direction]]
    shifted.append(jnp.where(y == 3, up(v, -3), up(v, 1)))
    shifted.append(jnp.where(y == 0, up(v, 3), up(v, -1)))
    return coarse_matrix([(ref, 96 * k, s) for k, s in enumerate(shifted)])


def load(ref, n, base=0):
    return [ref[base + i] for i in range(n)]


def store(ref, values, base=0):
    for i, x in enumerate(values):
        ref[base + i] = x


def finish_fine(site, links_ref, solution, sol_ref, acc_ref, pt_ref, pz_ref, mx_ref):
    store(sol_ref, solution)
    store(mx_ref, solution)
    fine_send(site, links_ref, solution, acc_ref, ((pt_ref, 0), (pz_ref, 0), (mx_ref, 6)))


def begin_fine(site, links_ref, refs):
    sol_ref, acc_ref, nz, bz, nt, bt, mx = refs
    solution = load(sol_ref, 6)
    ahead = [load(nt, 6), load(nz, 6), load(mx, 6)]
    behind = [load(bt, 6), load(bz, 6), load(mx, 6, 6)]
    return solution, fine_receive(site, links_ref, solution, load(acc_ref, 6), ahead, behind)


def kernel_first(links_ref, block_ref, rhs_ref, *outs):
    site = Site()
    solution = fine_matrix(site, block_ref, load(rhs_ref, 6))
    finish_fine(site, links_ref, solution, *outs)


def kernel_smooth(links_ref, block_ref, rhs_ref, *refs):
    site = Site()
    solution, applied = begin_fine(site, links_ref, refs[:7])
    residual = sub(load(rhs_ref, 6), applied)
    solution = add(solution, fine_matrix(site, block_ref, residual))
    finish_fine(site, links_ref, solution, *refs[7:])


def kernel_last(links_ref, rhs_ref, *refs):
    site = Site()
    _, applied = begin_fine(site, links_ref, refs[:7])
    store(refs[7], sub(load(rhs_ref, 6), applied))


def kernel_restrict(links_ref, near_ref, jacobi_ref, rhs_ref, *refs):
    site = Site()
    _, applied = begin_fine(site, links_ref, refs[:7])
    residual = sub(load(rhs_ref, 6), applied)
    mid_res = restrict_fine(site, near_ref, residual)
    store(refs[7], mid_res)
    store(refs[8], mid_matrix(site, jacobi_ref, mid_res))


def neighbours(refs, get):
    nz, bz, nt, bt = refs[:4]
    nx = refs[4]
    bx = refs[-1]
    ahead = [get(nt), get(nz), get(nx)]
    return ahead, [get(bt), get(bz), get(bx)]


def kernel_mid_down(stencil_ref, near_ref, jacobi_ref, res_ref, sol_ref, *refs):
    site = Site()
    around, (r3_ref, y3_ref, tile_ref) = refs[:-3], refs[-3:]
    ahead, behind = neighbours(around, lambda r: load(r, 3))
    applied = mid_stencil_apply(site, stencil_ref, load(sol_ref, 3), ahead, behind)
    r3 = restrict_mid(site, near_ref, sub(load(res_ref, 3), applied), tile_ref)
    r3_ref[...] = r3
    y3_ref[...] = coarse_matrix([(jacobi_ref, 0, r3)])


def sweep(stencil_ref, jacobi_ref, r3_ref, y3_ref, around):
    ahead, behind = neighbours(around, lambda r: r[...])
    y3 = y3_ref[...]
    rest = r3_ref[...] - coarse_stencil_apply(stencil_ref, y3, ahead, behind)
    return y3 + coarse_matrix([(jacobi_ref, 0, rest)])


def kernel_sweep(stencil_ref, jacobi_ref, r3_ref, y3_ref, *refs):
    refs[-1][...] = sweep(stencil_ref, jacobi_ref, r3_ref, y3_ref, refs[:-1])


def kernel_sweep_up(stencil_ref, jacobi_ref, near_ref, y2_ref, r3_ref, y3_ref, *refs):
    site = Site()
    around, (out_ref, row_ref) = refs[:-2], refs[-2:]
    y3 = sweep(stencil_ref, jacobi_ref, r3_ref, y3_ref, around)
    store(out_ref, add(load(y2_ref, 3), prolong_mid(site, near_ref, y3, row_ref)))


def kernel_mid_up(links_ref, stencil_ref, jacobi_ref, near_ref, old_ref, res_ref, y2_ref, *refs):
    site = Site()
    around, outs, spread_ref = refs[:-6], refs[-6:-1], refs[-1]
    ahead, behind = neighbours(around, lambda r: load(r, 3))
    y2 = load(y2_ref, 3)
    rest = sub(load(res_ref, 3), mid_stencil_apply(site, stencil_ref, y2, ahead, behind))
    y2 = add(y2, mid_matrix(site, jacobi_ref, rest))
    solution = add(load(old_ref, 6), prolong_fine(site, near_ref, y2, spread_ref))
    finish_fine(site, links_ref, solution, *outs)


def call(kernel, outs, scratch, *args):
    return pl.pallas_call(
        kernel,
        out_shape=[jax.ShapeDtypeStruct(s, F32) for s in outs],
        scratch_shapes=[pltpu.VMEM(s, F32) for s in scratch],
        compiler_params=pltpu.CompilerParams(vmem_limit_bytes=VMEM_BYTES),
        name=kernel.__name__,
    )(*args)


def from_behind(block, axis, distance):
    n = lax.axis_size(axis)
    return lax.ppermute(block, axis, [((i - distance) % n, i) for i in range(n)])


def exchange(v):
    around = [
        from_behind(v, "gz", -1),
        from_behind(v, "gz", 1),
        from_behind(v, "ta", -1),
        from_behind(v, "ta", 1),
        from_behind(v, "xy", -1),
    ]
    if lax.axis_size("xy") > 2:
        around.append(from_behind(v, "xy", 1))
    return around


def exchange_fine(sol, acc, pt, pz, mx):
    if lax.axis_size("xy") == 2:
        moved = from_behind(mx, "xy", 1)
    else:
        moved = jnp.concatenate([from_behind(mx[:6], "xy", -1), from_behind(mx[6:], "xy", 1)])
    return [
        sol,
        acc,
        from_behind(sol, "gz", -1),
        from_behind(pz, "gz", 1),
        from_behind(sol, "ta", -1),
        from_behind(pt, "ta", 1),
        moved,
    ]


TILE6 = (6, 8, 128)
FINE_OUT = [TILE6, TILE6, TILE6, TILE6, (12, 8, 128)]


def to_tiles(field):
    folded = field.reshape(6, 2, 2, 2, 2, 2, 2, 8, 2)
    return folded.transpose(0, 1, 3, 5, 2, 4, 6, 8, 7).reshape(TILE6)


def from_tiles(tiles, shape):
    folded = tiles.reshape(6, 2, 2, 2, 2, 2, 2, 2, 8)
    return folded.transpose(0, 1, 4, 2, 5, 3, 6, 8, 7).reshape(shape)


def link_tiles(links):
    folded = links.reshape(9, 2, 2, 2, 2, 2, 2, 16, 8, 2)
    tiles = folded.transpose(7, 0, 1, 3, 5, 2, 4, 6, 9, 8).reshape(4, 36, 8, 128).astype(F32)
    lane = lax.iota(jnp.int32, 128)
    ct, cz, cx = (lane >> 6) & 1, (lane >> 5) & 1, (lane >> 4) & 1
    odd = jnp.stack([0 * ct, ct, ct ^ cz, ct ^ cz ^ cx]).astype(F32)
    return (tiles * (0.5 - odd)[:, None, None, :]).reshape(144, 8, 128)


def local(
    right_side,
    links,
    block_inverse,
    near_fine,
    mid_stencil,
    mid_jacobi,
    near_mid,
    coarse_stencil,
    coarse_jacobi,
):
    g = link_tiles(links)
    rhs = to_tiles(right_side)
    block = block_inverse.reshape(384, 768)
    near1 = near_fine.reshape(192, 768)
    stencil2 = mid_stencil.reshape(1728, 384)
    jacobi2 = mid_jacobi.reshape(192, 384)
    near2 = near_mid.reshape(48, 48, 8, 2, 4).transpose(0, 2, 1, 4, 3).reshape(384, 384)
    stencil3 = jnp.swapaxes(coarse_stencil, 5, 6).reshape(864, 192)
    jacobi3 = jnp.swapaxes(coarse_jacobi, 4, 5).reshape(96, 192)
    mid = (3, 8, 128)
    coarse = (8, 48)

    state = call(kernel_first, FINE_OUT, [], g, block, rhs)
    for cycle_no in range(CYCLES):
        r2, y2 = call(kernel_restrict, [mid, mid], [], g, near1, jacobi2, rhs, *exchange_fine(*state))
        r3, y3 = call(
            kernel_mid_down, [coarse, coarse], [(2, 384, 128)], stencil2, near2, jacobi3, r2, y2, *exchange(y2)
        )
        for _ in range(SWEEPS - 1):
            (y3,) = call(kernel_sweep, [coarse], [], stencil3, jacobi3, r3, y3, *exchange(y3))
        (y2,) = call(
            kernel_sweep_up, [mid], [(2, 48, 128)], stencil3, jacobi3, near2, y2, r3, y3, *exchange(y3)
        )
        state = call(
            kernel_mid_up, FINE_OUT, [(48, 8, 128)], g, stencil2, jacobi2, near1, state[0], r2, y2, *exchange(y2)
        )
        state = call(kernel_smooth, FINE_OUT, [], g, block, rhs, *exchange_fine(*state))
        if cycle_no < CYCLES - 1:
            state = call(kernel_smooth, FINE_OUT, [], g, block, rhs, *exchange_fine(*state))
    (residual,) = call(kernel_last, [TILE6], [], g, rhs, *exchange_fine(*state))
    return from_tiles(state[0], right_side.shape), from_tiles(residual, right_side.shape)


def solution(mesh):
    return jax.shard_map(
        local,
        mesh=mesh,
        in_specs=(
            P(None, None, "ta", "gz", "xy", None),
            P(None, None, "ta", "gz", "xy", None),
            P(None, "ta", "gz", "xy", None),
            P(None, "ta", "gz", "xy", None),
            P(None, None, "ta", "gz", "xy", None),
            P(None, "ta", "gz", "xy", None),
            P(None, "ta", "gz", "xy", None),
            P(None, None, "ta", "gz", "xy", None, None),
            P(None, "ta", "gz", "xy", None, None),
        ),
        out_specs=(P(None, None, "ta", "gz", "xy", None), P(None, None, "ta", "gz", "xy", None)),
        check_vma=False,
    )
```

```python
import jax
import jax.numpy as jnp
from jax import lax
from jax.sharding import PartitionSpec as P
import jax.experimental.pallas as pl
from jax.experimental.pallas import tpu as pltpu

SWEEPS = 4
CYCLES = 2
F32 = jnp.float32
BF16 = jnp.bfloat16
HIGHEST = lax.Precision.HIGHEST
LANE_BITS = (64, 32, 16)
ROW_BITS = (4, 2, 1)
VMEM_BYTES = 24 << 20


class Site:
    def __init__(self):
        self.lane = lax.broadcasted_iota(jnp.int32, (8, 128), 1)
        self.row = lax.broadcasted_iota(jnp.int32, (8, 128), 0)
        self.by = self.lane & 7

    def lane_bit(self, d):
        return (self.lane & d) != 0

    def row_bit(self, d):
        return (self.row & d) != 0

    def first(self, direction):
        return ((self.lane & LANE_BITS[direction]) | (self.row & ROW_BITS[direction])) == 0

    def last(self, direction):
        return self.lane_bit(LANE_BITS[direction]) & self.row_bit(ROW_BITS[direction])


def left(x, s):
    s = s % 128
    return pltpu.roll(x, (128 - s) % 128, 1) if s else x


def up(x, s):
    s = s % 8
    return pltpu.roll(x, (8 - s) % 8, 0) if s else x


def flip_lane(site, x, d):
    if d == 64:
        return left(x, 64)
    return jnp.where(site.lane_bit(d), left(x, -d), left(x, d))


def flip_row(site, x, d):
    if d == 4:
        return up(x, 4)
    return jnp.where(site.row_bit(d), up(x, -d), up(x, d))


def cyclic(site, x, direction, sign):
    d = LANE_BITS[direction]
    flipped = flip_lane(site, x, d)
    both = flip_row(site, flipped, ROW_BITS[direction])
    if sign > 0:
        return jnp.where(site.lane_bit(d), both, flipped)
    return jnp.where(site.lane_bit(d), flipped, both)


def by_roll(site, x, base, q):
    moved = left(x, base + q)
    if q == 0:
        return moved
    if q > 0:
        return jnp.where(site.by >= 8 - q, left(x, base + q - 8), moved)
    return jnp.where(site.by < -q, left(x, base + q + 8), moved)


def shift_y(site, x, n):
    found = []
    for c in (0, 1):
        c_new = (c + n) % 2
        q = (c + n - c_new) // 2
        found.append(by_roll(site, x, 8 * (c_new - c), q))
    return jnp.where(site.lane_bit(8), found[1], found[0])


def link(links_ref, mu, kind, part, r, c):
    return links_ref[((mu * 2 + kind) * 2 + part) * 9 + r * 3 + c]


def link_apply(links_ref, mu, kind, field):
    out = [None] * 6
    for r in range(3):
        re = im = None
        for c in range(3):
            g_re = link(links_ref, mu, kind, 0, r, c)
            g_im = link(links_ref, mu, kind, 1, r, c)
            a = g_re * field[c] - g_im * field[3 + c]
            b = g_re * field[3 + c] + g_im * field[c]
            re = a if re is None else re + a
            im = b if im is None else im + b
        out[r] = re
        out[3 + r] = im
    return out


def link_adjoint(links_ref, mu, kind, field):
    out = [None] * 6
    for c in range(3):
        re = im = None
        for r in range(3):
            g_re = link(links_ref, mu, kind, 0, r, c)
            g_im = link(links_ref, mu, kind, 1, r, c)
            a = g_re * field[r] + g_im * field[3 + r]
            b = g_re * field[3 + r] - g_im * field[r]
            re = a if re is None else re + a
            im = b if im is None else im + b
        out[c] = re
        out[3 + c] = im
    return out


def add(xs, ys):
    return [x + y for x, y in zip(xs, ys)]


def sub(xs, ys):
    return [x - y for x, y in zip(xs, ys)]


def fine_send(site, links_ref, field, acc_ref):
    acc = list(field)
    for kind, reach in ((0, 1), (1, 3)):
        acc = add(acc, link_apply(links_ref, 3, kind, [shift_y(site, x, reach) for x in field]))
        back = link_adjoint(links_ref, 3, kind, field)
        acc = sub(acc, [shift_y(site, x, -reach) for x in back])
    sent = []
    for direction in range(3):
        near = [cyclic(site, x, direction, -1) for x in link_adjoint(links_ref, direction, 0, field)]
        far = link_adjoint(links_ref, direction, 1, field)
        first, last = site.first(direction), site.last(direction)
        sent.append([jnp.where(first, n, f) for n, f in zip(near, far)])
        acc = [
            a - jnp.where(first, 0.0, n) - jnp.where(last, cyclic(site, f, direction, 1), 0.0)
            for a, n, f in zip(acc, near, far)
        ]
    for i in range(6):
        acc_ref[i] = acc[i]
    return sent


def fine_receive(site, links_ref, field, acc, ahead, behind):
    out = acc
    for direction in range(3):
        first, last = site.first(direction), site.last(direction)
        nxt = ahead[direction]
        one = [cyclic(site, jnp.where(first, n, x), direction, 1) for n, x in zip(nxt, field)]
        out = add(out, link_apply(links_ref, direction, 0, one))
        three = [cyclic(site, jnp.where(last, x, n), direction, -1) for n, x in zip(nxt, field)]
        out = add(out, link_apply(links_ref, direction, 1, three))
        out = [
            o - jnp.where(first, b, 0.0) - jnp.where(last, 0.0, cyclic(site, b, direction, 1))
            for o, b in zip(out, behind[direction])
        ]
    return out


def merge(site, d, a, b):
    bit = site.lane_bit(d)
    return jnp.where(bit, b, a) + left(jnp.where(bit, a, b), d)


def tree(site, leaf, base, n):
    if n == 2:
        a, b = leaf(base)
    else:
        a = tree(site, leaf, base, n // 2)
        b = tree(site, leaf, base + n // 2, n // 2)
    return [merge(site, 4 * n, x, y) for x, y in zip(a, b)]


def two_rows(ref, o):
    return ref[pl.ds(o * 8, 16), :].astype(F32)


def dot_tiles(block, row, x):
    total = None
    for j, v in enumerate(x):
        term = block[row : row + 8, 128 * j : 128 * j + 128] * v
        total = term if total is None else total + term
    return total


def pair_leaf(terms):
    def leaf(o):
        sums = [[None, None], [None, None]]
        for ref, base, x_re, x_im in terms:
            block = two_rows(ref, base + o)
            for h in range(2):
                for p, x in enumerate((x_re, x_im)):
                    t = dot_tiles(block, 8 * h, x)
                    sums[h][p] = t if sums[h][p] is None else sums[h][p] + t
        return sums

    return leaf


def fine_matrix(site, ref, field):
    x_re = field[:3] + [-x for x in field[3:]]
    x_im = field[3:] + field[:3]
    out = [tree(site, pair_leaf([(ref, 0, x_re, x_im)]), 16 * c, 16) for c in range(3)]
    return [o[0] for o in out] + [o[1] for o in out]


def mid_gather(site, terms):
    leaf = pair_leaf(terms)
    eight = [tree(site, leaf, 8 * j, 8) for j in range(3)]
    return [
        merge(site, 64, eight[0][0], eight[1][0]),
        merge(site, 64, eight[2][0], eight[0][1]),
        merge(site, 64, eight[1][1], eight[2][1]),
    ]


def swap_parts(site, v):
    low = jnp.logical_not(site.lane_bit(64))
    r = [left(x, 64) for x in v]
    return [jnp.where(low, r[1], r[2]), jnp.where(low, r[2], r[0]), jnp.where(low, r[0], r[1])]


def im_negated(site, v):
    return [v[0], jnp.where(site.lane_bit(64), -v[1], v[1]), -v[2]]


def mid_x(site, v):
    return im_negated(site, v), swap_parts(site, v)


def mid_x_conj(site, v):
    return v, im_negated(site, swap_parts(site, v))


def restrict_fine(site, near_ref, field):
    x_im = field[3:] + [-x for x in field[:3]]
    return mid_gather(site, [(near_ref, 0, field, x_im)])


def mid_matrix(site, ref, v):
    x_re, x_im = mid_x(site, v)
    return mid_gather(site, [(ref, 0, x_re, x_im)])


def mid_stencil_apply(site, ref, v, ahead, behind):
    shifted = [v]
    for direction in range(3):
        d = ROW_BITS[direction]
        bit = site.row_bit(d)
        shifted.append([flip_row(site, jnp.where(bit, x, n), d) for x, n in zip(v, ahead[direction])])
        shifted.append([flip_row(site, jnp.where(bit, n, x), d) for x, n in zip(v, behind[direction])])
    shifted.append([by_roll(site, x, 0, 1) for x in v])
    shifted.append([by_roll(site, x, 0, -1) for x in v])
    return mid_gather(site, [(ref, 24 * k) + mid_x(site, s) for k, s in enumerate(shifted)])


def spread(site, v, ref):
    def down(x, base, d):
        if d == 4:
            ref[base] = x
            return
        bit = site.lane_bit(d)
        r = left(x, d)
        down(jnp.where(bit, r, x), base, d // 2)
        down(jnp.where(bit, x, r), base + d // 8, d // 2)

    for j, x in enumerate(v):
        down(x, 16 * j, 64)


def prolong_fine(site, near_ref, v, spread_ref):
    spread(site, v, spread_ref)
    a, b = [0.0] * 6, [0.0] * 6
    for o in range(0, 24, 2):
        block = two_rows(near_ref, o)
        for h in range(2):
            y_re, y_im = spread_ref[o + h], spread_ref[24 + o + h]
            for j in range(6):
                n = block[8 * h : 8 * h + 8, 128 * j : 128 * j + 128]
                a[j] = a[j] + n * y_re
                b[j] = b[j] + n * y_im
    return [a[j] - b[3 + j] for j in range(3)] + [a[3 + j] + b[j] for j in range(3)]


def iota2(shape, axis):
    return lax.broadcasted_iota(jnp.int32, shape, axis)


def pick_y(part):
    row, lane = iota2((8, 128), 0), iota2((8, 128), 1)
    return (row == part * 4 + (lane & 3)).astype(F32)


def permute_eight(site, x, source):
    out = x
    for move in sorted({s - i for i, s in enumerate(source)} - {0}):
        hit = None
        for i, s in enumerate(source):
            if s - i == move:
                hit = (site.by == i) if hit is None else hit | (site.by == i)
        out = jnp.where(hit, left(x, move), out)
    return out


SPLIT_Y = (0, 2, 4, 6, 1, 3, 5, 7)
JOIN_Y = (0, 4, 1, 5, 2, 6, 3, 7)


def total_rows(x):
    for d in (4, 2, 1):
        x = x + up(x, d)
    return x


def widen(site, v):
    own = ((site.lane >> 3) & 7) == site.row
    half = site.lane_bit(64) == site.lane_bit(8)
    found = []

    def down(x, d):
        if d == 8:
            x = jnp.where(half, x, flip_lane(site, x, 8))
            found.append(total_rows(jnp.where(own, x, 0.0)))
            return
        bit = site.lane_bit(d)
        r = left(x, d)
        down(jnp.where(bit, r, x), d // 2)
        down(jnp.where(bit, x, r), d // 2)

    for x in v:
        down(permute_eight(site, x, SPLIT_Y), 64)
    return found


def narrow(site, tiles):
    own = ((site.lane >> 3) & 7) == site.row
    same = site.lane_bit(64) == site.lane_bit(8)

    def fold(d, a, b):
        bit = site.lane_bit(d)
        return jnp.where(bit, b, a) + flip_lane(site, jnp.where(bit, a, b), d)

    out = []
    for q in range(0, 24, 8):
        t = [jnp.where(own, total_rows(x), 0.0) for x in tiles[q : q + 8]]
        t = [fold(8, t[i], t[i + 4]) for i in range(4)]
        t = [fold(32, t[i], t[i + 2]) for i in range(2)]
        x = fold(16, t[0], t[1])
        x = jnp.where(same, x, jnp.where(site.lane_bit(64), left(x, -56), left(x, 56)))
        out.append(permute_eight(site, x, JOIN_Y))
    return out


def restrict_mid(site, near_ref, v, tile_ref):
    x = widen(site, v)
    x_im = x[12:] + [-t for t in x[:12]]
    for o in range(0, 48, 16):
        re = [None, None]
        im = [None, None]
        for j in range(24):
            n = near_ref[pl.ds(o, 16), pl.ds(128 * j, 128)].astype(F32)
            for h in range(2):
                block = n[8 * h : 8 * h + 8]
                a, b = block * x[j], block * x_im[j]
                re[h] = a if re[h] is None else re[h] + a
                im[h] = b if im[h] is None else im[h] + b
        for h in range(2):
            tile_ref[0, pl.ds(o + 8 * h, 8), :] = re[h]
            tile_ref[1, pl.ds(o + 8 * h, 8), :] = im[h]
    dims = (((1,), (1,)), ((), ()))
    z = None
    for p in range(2):
        t = lax.dot_general(pick_y(p), tile_ref[p], dims, precision=HIGHEST, preferred_element_type=F32)
        z = t if z is None else z + t
    return z


def prolong_mid(site, near_ref, y3, row_ref):
    dims = (((0,), (0,)), ((), ()))
    for p in range(2):
        row_ref[p] = lax.dot_general(y3, pick_y(p), dims, precision=HIGHEST, preferred_element_type=F32)
    a, b = [None] * 24, [None] * 24
    for j in range(24):
        for o in range(0, 48, 16):
            n = near_ref[pl.ds(o, 16), pl.ds(128 * j, 128)].astype(F32)
            for h in range(2):
                block = n[8 * h : 8 * h + 8]
                s = block * row_ref[0, pl.ds(o + 8 * h, 8), :]
                t = block * row_ref[1, pl.ds(o + 8 * h, 8), :]
                a[j] = s if a[j] is None else a[j] + s
                b[j] = t if b[j] is None else b[j] + t
    tiles = [a[j] - b[12 + j] for j in range(12)] + [a[12 + j] + b[j] for j in range(12)]
    return narrow(site, tiles)


def coarse_rows(v):
    high = v.astype(BF16).astype(F32)
    return jnp.concatenate([high, v - high], axis=0).astype(BF16)


def coarse_matrix(terms):
    row = iota2((8, 48), 0)
    total = None
    for ref, base, v in terms:
        turned = jnp.where(row < 4, -up(v, 4), up(v, 4))
        for a, x in enumerate((v, turned)):
            t = jnp.dot(coarse_rows(x), ref[pl.ds(base + 48 * a, 48), :], preferred_element_type=F32)
            total = t if total is None else total + t
    both = total[:8] + total[8:]
    out = None
    for y in range(4):
        t = jnp.where((row & 3) == y, both[:, 48 * y : 48 * y + 48], 0.0)
        out = t if out is None else out + t
    return out


def coarse_stencil_apply(ref, v, ahead, behind):
    y = iota2((8, 48), 0) & 3
    shifted = [v]
    for direction in range(3):
        shifted += [ahead[direction], behind[direction]]
    shifted.append(jnp.where(y == 3, up(v, -3), up(v, 1)))
    shifted.append(jnp.where(y == 0, up(v, 3), up(v, -1)))
    return coarse_matrix([(ref, 96 * k, s) for k, s in enumerate(shifted)])


def load(ref, n, base=0):
    return [ref[base + i] for i in range(n)]


def store(ref, values, base=0):
    for i, x in enumerate(values):
        ref[base + i] = x


def is_odd(axis):
    return lax.rem(lax.axis_index(axis), 2) == 1


def finish_fine(site, links_ref, solution, sol_ref, acc_ref, z0_ref, z1_ref, t0_ref, t1_ref, x_ref):
    store(sol_ref, solution)
    store(x_ref, solution)
    back_t, back_z, back_x = fine_send(site, links_ref, solution, acc_ref)
    store(x_ref, back_x, 6)
    for axis, back, ref0, ref1 in (("gz", back_z, z0_ref, z1_ref), ("ta", back_t, t0_ref, t1_ref)):
        odd = is_odd(axis)
        store(ref0, [jnp.where(odd, s, b) for s, b in zip(solution, back)])
        store(ref1, [jnp.where(odd, b, s) for s, b in zip(solution, back)])


def by_parity(axis, zero, one):
    odd = is_odd(axis)
    ahead = [jnp.where(odd, b, a) for a, b in zip(zero, one)]
    return ahead, [jnp.where(odd, a, b) for a, b in zip(zero, one)]


def begin_fine(site, links_ref, refs):
    sol_ref, acc_ref, z1, t1, x, z0, t0 = refs
    solution = load(sol_ref, 6)
    ahead_t, behind_t = by_parity("ta", load(t0, 6), load(t1, 6))
    ahead_z, behind_z = by_parity("gz", load(z0, 6), load(z1, 6))
    ahead = [ahead_t, ahead_z, load(x, 6)]
    behind = [behind_t, behind_z, load(x, 6, 6)]
    return solution, fine_receive(site, links_ref, solution, load(acc_ref, 6), ahead, behind)


def row_order(transposed):
    m, n = iota2((64, 64), 0), iota2((64, 64), 1)
    if transposed:
        m, n = n, m
    bit = lambda v, k: (v >> k) & 1
    fine = (
        (bit(m, 2) << 5) | (bit(m, 5) << 4) | (bit(m, 1) << 3) | (bit(m, 4) << 2) | (bit(m, 0) << 1) | bit(m, 3)
    )
    return n == fine


def y_order(rows, columns, transposed):
    m, n = iota2((rows, columns), 0), iota2((rows, columns), 1)
    if transposed:
        m, n = n, m
    fine = (((n & 7) << 1) | ((n >> 3) & 1)) | (n & 112)
    return m == (fine & (min(rows, columns) - 1))


def exact_dot(a, b):
    return jnp.dot(a, b, precision=HIGHEST, preferred_element_type=F32)


def prepare_links(site, links_ref, g_ref):
    rows = row_order(False).astype(BF16)
    lanes = y_order(128, 128, False).astype(BF16)
    signs = [jnp.full((8, 128), 0.5, F32)]
    for d in LANE_BITS:
        signs.append(jnp.where(site.lane_bit(d), -signs[-1], signs[-1]))
    for rc in range(9):
        block = links_ref[pl.ds(64 * rc, 64), :]
        block = jnp.dot(rows, block, preferred_element_type=F32).astype(BF16)
        for h in range(2):
            half = jnp.dot(block[:, 128 * h : 128 * h + 128], lanes, preferred_element_type=F32)
            v = [half[8 * w : 8 * w + 8] for w in range(8)]
            for d, k in zip(LANE_BITS, (4, 2, 1)):
                bit = site.lane_bit(d)
                for w in range(8):
                    if not w & k:
                        lo, hi = v[w], v[w | k]
                        v[w] = jnp.where(bit, left(hi, -d), lo)
                        v[w | k] = jnp.where(bit, hi, left(lo, d))
            for m in range(8):
                g_ref[(8 * h + m) * 9 + rc] = v[m] * signs[2 * h + m // 4]


def gather_fine(site, field_ref):
    rows = row_order(False).astype(F32)
    lanes = y_order(16, 128, False).astype(F32)
    group = site.lane >> 4
    out = []
    for p in range(2):
        for c in range(3):
            parts = [field_ref[p, c, t, z] for t in range(4) for z in range(4)]
            spread_out = exact_dot(rows, exact_dot(jnp.concatenate(parts, axis=0), lanes))
            total = spread_out[:8]
            for w in range(1, 8):
                total = jnp.where(group == w, spread_out[8 * w : 8 * w + 8], total)
            out.append(total)
    return out


def scatter_fine(site, field, out_ref):
    rows = row_order(True).astype(F32)
    lanes = y_order(128, 16, True).astype(F32)
    group = site.lane >> 4
    for p in range(2):
        for c in range(3):
            x = field[3 * p + c]
            tall = jnp.concatenate([jnp.where(group == w, x, 0.0) for w in range(8)], axis=0)
            value = exact_dot(rows, exact_dot(tall, lanes))
            for t in range(4):
                for z in range(4):
                    out_ref[p, c, t, z] = value[16 * t + 4 * z : 16 * t + 4 * z + 4]


def kernel_first(links_ref, block_ref, source_ref, g_ref, rhs_ref, *outs):
    site = Site()
    rhs = gather_fine(site, source_ref)
    store(rhs_ref, rhs)
    prepare_links(site, links_ref, g_ref)
    finish_fine(site, g_ref, fine_matrix(site, block_ref, rhs), *outs)


def kernel_smooth(links_ref, block_ref, rhs_ref, *refs):
    site = Site()
    solution, applied = begin_fine(site, links_ref, refs[:7])
    residual = sub(load(rhs_ref, 6), applied)
    solution = add(solution, fine_matrix(site, block_ref, residual))
    finish_fine(site, links_ref, solution, *refs[7:])


def kernel_last(links_ref, rhs_ref, *refs):
    site = Site()
    solution, applied = begin_fine(site, links_ref, refs[:7])
    scatter_fine(site, solution, refs[7])
    scatter_fine(site, sub(load(rhs_ref, 6), applied), refs[8])


def kernel_restrict(links_ref, near_ref, jacobi_ref, rhs_ref, *refs):
    site = Site()
    _, applied = begin_fine(site, links_ref, refs[:7])
    residual = sub(load(rhs_ref, 6), applied)
    mid_res = restrict_fine(site, near_ref, residual)
    store(refs[7], mid_res)
    store(refs[8], mid_matrix(site, jacobi_ref, mid_res))


def neighbours(refs, get):
    z1, t1, nx, z0, t0 = refs[:5]
    ahead_t, behind_t = by_parity("ta", get(t0), get(t1))
    ahead_z, behind_z = by_parity("gz", get(z0), get(z1))
    return [ahead_t, ahead_z, get(nx)], [behind_t, behind_z, get(refs[-1] if len(refs) > 5 else nx)]


def kernel_mid_down(stencil_ref, near_ref, jacobi_ref, res_ref, sol_ref, *refs):
    site = Site()
    around, (r3_ref, y3_ref, tile_ref) = refs[:-3], refs[-3:]
    ahead, behind = neighbours(around, lambda r: load(r, 3))
    applied = mid_stencil_apply(site, stencil_ref, load(sol_ref, 3), ahead, behind)
    r3 = restrict_mid(site, near_ref, sub(load(res_ref, 3), applied), tile_ref)
    r3_ref[...] = r3
    y3_ref[...] = coarse_matrix([(jacobi_ref, 0, r3)])


def sweep(stencil_ref, jacobi_ref, r3_ref, y3_ref, around):
    ahead, behind = neighbours(around, lambda r: [r[...]])
    ahead, behind = [x[0] for x in ahead], [x[0] for x in behind]
    y3 = y3_ref[...]
    rest = r3_ref[...] - coarse_stencil_apply(stencil_ref, y3, ahead, behind)
    return y3 + coarse_matrix([(jacobi_ref, 0, rest)])


def kernel_sweep(stencil_ref, jacobi_ref, r3_ref, y3_ref, *refs):
    refs[-1][...] = sweep(stencil_ref, jacobi_ref, r3_ref, y3_ref, refs[:-1])


def kernel_sweep_up(stencil_ref, jacobi_ref, near_ref, y2_ref, r3_ref, y3_ref, *refs):
    site = Site()
    around, (out_ref, row_ref) = refs[:-2], refs[-2:]
    y3 = sweep(stencil_ref, jacobi_ref, r3_ref, y3_ref, around)
    store(out_ref, add(load(y2_ref, 3), prolong_mid(site, near_ref, y3, row_ref)))


def kernel_mid_up(links_ref, stencil_ref, jacobi_ref, near_ref, old_ref, res_ref, y2_ref, *refs):
    site = Site()
    around, outs, spread_ref = refs[:-8], refs[-8:-1], refs[-1]
    ahead, behind = neighbours(around, lambda r: load(r, 3))
    y2 = load(y2_ref, 3)
    rest = sub(load(res_ref, 3), mid_stencil_apply(site, stencil_ref, y2, ahead, behind))
    y2 = add(y2, mid_matrix(site, jacobi_ref, rest))
    solution = add(load(old_ref, 6), prolong_fine(site, near_ref, y2, spread_ref))
    finish_fine(site, links_ref, solution, *outs)


def call(kernel, outs, scratch, *args):
    return pl.pallas_call(
        kernel,
        out_shape=[jax.ShapeDtypeStruct(s, F32) for s in outs],
        scratch_shapes=[pltpu.VMEM(s, F32) for s in scratch],
        compiler_params=pltpu.CompilerParams(vmem_limit_bytes=VMEM_BYTES),
        name=kernel.__name__,
    )(*args)


def from_behind(block, axis, distance):
    n = lax.axis_size(axis)
    return lax.ppermute(block, axis, [((i - distance) % n, i) for i in range(n)])


def swap(block, axis, phase):
    n = lax.axis_size(axis)
    return lax.ppermute(block, axis, [(i, (((i + phase) ^ 1) - phase) % n) for i in range(n)])


def exchange(v):
    z1 = swap(v, "gz", 1)
    t1 = swap(v, "ta", 1)
    x = from_behind(v, "xy", -1)
    z0 = swap(v, "gz", 0)
    t0 = swap(v, "ta", 0)
    return [z1, t1, x, z0, t0] + ([from_behind(v, "xy", 1)] if lax.axis_size("xy") > 2 else [])


def exchange_fine(sol, acc, z0, z1, t0, t1, x):
    z1 = swap(z1, "gz", 1)
    t1 = swap(t1, "ta", 1)
    if lax.axis_size("xy") == 2:
        x = from_behind(x, "xy", 1)
    else:
        x = jnp.concatenate([from_behind(x[:6], "xy", -1), from_behind(x[6:], "xy", 1)])
    return [sol, acc, z1, t1, x, swap(z0, "gz", 0), swap(t0, "ta", 0)]


TILE6 = (6, 8, 128)
FINE_OUT = [TILE6] * 6 + [(12, 8, 128)]


def local(
    right_side,
    links,
    block_inverse,
    near_fine,
    mid_stencil,
    mid_jacobi,
    near_mid,
    coarse_stencil,
    coarse_jacobi,
):
    links_flat = links.reshape(576, 256)
    block = block_inverse.reshape(384, 768)
    near1 = near_fine.reshape(192, 768)
    stencil2 = mid_stencil.reshape(1728, 384)
    jacobi2 = mid_jacobi.reshape(192, 384)
    near2 = near_mid.reshape(near_mid.shape[0], near_mid.shape[4])
    stencil3 = jnp.swapaxes(coarse_stencil, 5, 6).reshape(864, 192)
    jacobi3 = jnp.swapaxes(coarse_jacobi, 4, 5).reshape(96, 192)
    mid = (3, 8, 128)
    coarse = (8, 48)

    g, rhs, *state = call(kernel_first, [(144, 8, 128), TILE6] + FINE_OUT, [], links_flat, block, right_side)
    for cycle_no in range(CYCLES):
        r2, y2 = call(kernel_restrict, [mid, mid], [], g, near1, jacobi2, rhs, *exchange_fine(*state))
        r3, y3 = call(
            kernel_mid_down, [coarse, coarse], [(2, 48, 128)], stencil2, near2, jacobi3, r2, y2, *exchange(y2)
        )
        for _ in range(SWEEPS - 1):
            (y3,) = call(kernel_sweep, [coarse], [], stencil3, jacobi3, r3, y3, *exchange(y3))
        (y2,) = call(
            kernel_sweep_up, [mid], [(2, 48, 128)], stencil3, jacobi3, near2, y2, r3, y3, *exchange(y3)
        )
        state = call(
            kernel_mid_up, FINE_OUT, [(48, 8, 128)], g, stencil2, jacobi2, near1, state[0], r2, y2, *exchange(y2)
        )
        state = call(kernel_smooth, FINE_OUT, [], g, block, rhs, *exchange_fine(*state))
        if cycle_no < CYCLES - 1:
            state = call(kernel_smooth, FINE_OUT, [], g, block, rhs, *exchange_fine(*state))
    return call(kernel_last, [right_side.shape] * 2, [], g, rhs, *exchange_fine(*state))


def solution(mesh):
    return jax.shard_map(
        local,
        mesh=mesh,
        in_specs=(
            P(None, None, "ta", "gz", "xy", None),
            P(None, None, "ta", "gz", "xy", None),
            P(None, "ta", "gz", "xy", None),
            P(None, "ta", "gz", "xy", None),
            P(None, None, "ta", "gz", "xy", None),
            P(None, "ta", "gz", "xy", None),
            P(None, "ta", "gz", "xy", None),
            P(None, None, "ta", "gz", "xy", None, None),
            P(None, "ta", "gz", "xy", None, None),
        ),
        out_specs=(P(None, None, "ta", "gz", "xy", None), P(None, None, "ta", "gz", "xy", None)),
        check_vma=False,
    )
```

```python
import jax
import jax.numpy as jnp
from jax import lax
from jax.sharding import PartitionSpec as P
import jax.experimental.pallas as pl
from jax.experimental.pallas import tpu as pltpu

SWEEPS = 4
CYCLES = 2
F32 = jnp.float32
BF16 = jnp.bfloat16
HIGHEST = lax.Precision.HIGHEST
LANE_BITS = (64, 32, 16)
ROW_BITS = (4, 2, 1)
VMEM_BYTES = 24 << 20


class Site:
    def __init__(self):
        self.lane = lax.broadcasted_iota(jnp.int32, (8, 128), 1)
        self.row = lax.broadcasted_iota(jnp.int32, (8, 128), 0)
        self.by = self.lane & 7

    def lane_bit(self, d):
        return (self.lane & d) != 0

    def row_bit(self, d):
        return (self.row & d) != 0

    def first(self, direction):
        return ((self.lane & LANE_BITS[direction]) | (self.row & ROW_BITS[direction])) == 0

    def last(self, direction):
        return self.lane_bit(LANE_BITS[direction]) & self.row_bit(ROW_BITS[direction])


def left(x, s):
    s = s % 128
    return pltpu.roll(x, (128 - s) % 128, 1) if s else x


def up(x, s):
    s = s % 8
    return pltpu.roll(x, (8 - s) % 8, 0) if s else x


def flip_lane(site, x, d):
    if d == 64:
        return left(x, 64)
    return jnp.where(site.lane_bit(d), left(x, -d), left(x, d))


def flip_row(site, x, d):
    if d == 4:
        return up(x, 4)
    return jnp.where(site.row_bit(d), up(x, -d), up(x, d))


def cyclic(site, x, direction, sign):
    d = LANE_BITS[direction]
    flipped = flip_lane(site, x, d)
    both = flip_row(site, flipped, ROW_BITS[direction])
    if sign > 0:
        return jnp.where(site.lane_bit(d), both, flipped)
    return jnp.where(site.lane_bit(d), flipped, both)


def by_roll(site, x, base, q):
    moved = left(x, base + q)
    if q == 0:
        return moved
    if q > 0:
        return jnp.where(site.by >= 8 - q, left(x, base + q - 8), moved)
    return jnp.where(site.by < -q, left(x, base + q + 8), moved)


def shift_y(site, x, n):
    found = []
    for c in (0, 1):
        c_new = (c + n) % 2
        q = (c + n - c_new) // 2
        found.append(by_roll(site, x, 8 * (c_new - c), q))
    return jnp.where(site.lane_bit(8), found[1], found[0])


def link(links_ref, mu, kind, part, r, c):
    return links_ref[((mu * 2 + kind) * 2 + part) * 9 + r * 3 + c]


def link_apply(links_ref, mu, kind, field):
    out = [None] * 6
    for r in range(3):
        re = im = None
        for c in range(3):
            g_re = link(links_ref, mu, kind, 0, r, c)
            g_im = link(links_ref, mu, kind, 1, r, c)
            a = g_re * field[c] - g_im * field[3 + c]
            b = g_re * field[3 + c] + g_im * field[c]
            re = a if re is None else re + a
            im = b if im is None else im + b
        out[r] = re
        out[3 + r] = im
    return out


def link_adjoint(links_ref, mu, kind, field):
    out = [None] * 6
    for c in range(3):
        re = im = None
        for r in range(3):
            g_re = link(links_ref, mu, kind, 0, r, c)
            g_im = link(links_ref, mu, kind, 1, r, c)
            a = g_re * field[r] + g_im * field[3 + r]
            b = g_re * field[3 + r] - g_im * field[r]
            re = a if re is None else re + a
            im = b if im is None else im + b
        out[c] = re
        out[3 + c] = im
    return out


def add(xs, ys):
    return [x + y for x, y in zip(xs, ys)]


def sub(xs, ys):
    return [x - y for x, y in zip(xs, ys)]


def fine_send(site, links_ref, field, acc_ref):
    acc = list(field)
    for kind, reach in ((0, 1), (1, 3)):
        acc = add(acc, link_apply(links_ref, 3, kind, [shift_y(site, x, reach) for x in field]))
        back = link_adjoint(links_ref, 3, kind, field)
        acc = sub(acc, [shift_y(site, x, -reach) for x in back])
    sent = []
    for direction in range(3):
        near, far = backward(site, links_ref, field, direction)
        first, last = site.first(direction), site.last(direction)
        if direction < 2:
            sent.append([jnp.where(first, n, f) for n, f in zip(near, far)])
        acc = [
            a - jnp.where(first, 0.0, n) - jnp.where(last, cyclic(site, f, direction, 1), 0.0)
            for a, n, f in zip(acc, near, far)
        ]
    for i in range(6):
        acc_ref[i] = acc[i]
    return sent


class PairedLinks:
    def __init__(self, ref):
        self.ref = ref

    def __getitem__(self, i):
        i -= 72
        return self.ref[i // 2].astype(F32)[8 * (i % 2) : 8 * (i % 2) + 8]


def backward(site, links_ref, field, direction):
    near = [cyclic(site, x, direction, -1) for x in link_adjoint(links_ref, direction, 0, field)]
    return near, link_adjoint(links_ref, direction, 1, field)


def fine_receive(site, links_ref, field, acc, ahead, behind):
    out = acc
    for direction in range(3):
        first, last = site.first(direction), site.last(direction)
        nxt = ahead[direction]
        one = [cyclic(site, jnp.where(first, n, x), direction, 1) for n, x in zip(nxt, field)]
        out = add(out, link_apply(links_ref, direction, 0, one))
        three = [cyclic(site, jnp.where(last, x, n), direction, -1) for n, x in zip(nxt, field)]
        out = add(out, link_apply(links_ref, direction, 1, three))
        out = [
            o - jnp.where(first, b, 0.0) - jnp.where(last, 0.0, cyclic(site, b, direction, 1))
            for o, b in zip(out, behind[direction])
        ]
    return out


def merge(site, d, a, b):
    bit = site.lane_bit(d)
    return jnp.where(bit, b, a) + left(jnp.where(bit, a, b), d)


def tree(site, leaf, base, n):
    if n == 2:
        a, b = leaf(base)
    else:
        a = tree(site, leaf, base, n // 2)
        b = tree(site, leaf, base + n // 2, n // 2)
    return [merge(site, 4 * n, x, y) for x, y in zip(a, b)]


def two_rows(ref, o):
    return ref[pl.ds(o * 8, 16), :].astype(F32)


def dot_tiles(block, row, x):
    total = None
    for j, v in enumerate(x):
        term = block[row : row + 8, 128 * j : 128 * j + 128] * v
        total = term if total is None else total + term
    return total


def pair_leaf(terms):
    def leaf(o):
        sums = [[None, None], [None, None]]
        for ref, base, x_re, x_im in terms:
            block = two_rows(ref, base + o)
            for h in range(2):
                for p, x in enumerate((x_re, x_im)):
                    t = dot_tiles(block, 8 * h, x)
                    sums[h][p] = t if sums[h][p] is None else sums[h][p] + t
        return sums

    return leaf


def fine_matrix(site, ref, field):
    x_re = field[:3] + [-x for x in field[3:]]
    x_im = field[3:] + field[:3]
    out = [tree(site, pair_leaf([(ref, 0, x_re, x_im)]), 16 * c, 16) for c in range(3)]
    return [o[0] for o in out] + [o[1] for o in out]


def mid_gather(site, terms):
    leaf = pair_leaf(terms)
    eight = [tree(site, leaf, 8 * j, 8) for j in range(3)]
    return [
        merge(site, 64, eight[0][0], eight[1][0]),
        merge(site, 64, eight[2][0], eight[0][1]),
        merge(site, 64, eight[1][1], eight[2][1]),
    ]


def swap_parts(site, v):
    low = jnp.logical_not(site.lane_bit(64))
    r = [left(x, 64) for x in v]
    return [jnp.where(low, r[1], r[2]), jnp.where(low, r[2], r[0]), jnp.where(low, r[0], r[1])]


def im_negated(site, v):
    return [v[0], jnp.where(site.lane_bit(64), -v[1], v[1]), -v[2]]


def mid_x(site, v):
    return im_negated(site, v), swap_parts(site, v)


def mid_x_conj(site, v):
    return v, im_negated(site, swap_parts(site, v))


def restrict_fine(site, near_ref, field):
    x_im = field[3:] + [-x for x in field[:3]]
    return mid_gather(site, [(near_ref, 0, field, x_im)])


def mid_matrix(site, ref, v):
    x_re, x_im = mid_x(site, v)
    return mid_gather(site, [(ref, 0, x_re, x_im)])


def mid_stencil_apply(site, ref, v, ahead, behind):
    shifted = [v]
    for direction in range(3):
        d = ROW_BITS[direction]
        bit = site.row_bit(d)
        shifted.append([flip_row(site, jnp.where(bit, x, n), d) for x, n in zip(v, ahead[direction])])
        shifted.append([flip_row(site, jnp.where(bit, n, x), d) for x, n in zip(v, behind[direction])])
    shifted.append([by_roll(site, x, 0, 1) for x in v])
    shifted.append([by_roll(site, x, 0, -1) for x in v])
    return mid_gather(site, [(ref, 24 * k) + mid_x(site, s) for k, s in enumerate(shifted)])


def spread(site, v, ref):
    def down(x, base, d):
        if d == 4:
            ref[base] = x
            return
        bit = site.lane_bit(d)
        r = left(x, d)
        down(jnp.where(bit, r, x), base, d // 2)
        down(jnp.where(bit, x, r), base + d // 8, d // 2)

    for j, x in enumerate(v):
        down(x, 16 * j, 64)


def prolong_fine(site, near_ref, v, spread_ref):
    spread(site, v, spread_ref)
    a, b = [0.0] * 6, [0.0] * 6
    for o in range(0, 24, 2):
        block = two_rows(near_ref, o)
        for h in range(2):
            y_re, y_im = spread_ref[o + h], spread_ref[24 + o + h]
            for j in range(6):
                n = block[8 * h : 8 * h + 8, 128 * j : 128 * j + 128]
                a[j] = a[j] + n * y_re
                b[j] = b[j] + n * y_im
    return [a[j] - b[3 + j] for j in range(3)] + [a[3 + j] + b[j] for j in range(3)]


def iota2(shape, axis):
    return lax.broadcasted_iota(jnp.int32, shape, axis)


def pick_y(part):
    row, lane = iota2((8, 128), 0), iota2((8, 128), 1)
    return (row == part * 4 + (lane & 3)).astype(F32)


def permute_eight(site, x, source):
    out = x
    for move in sorted({s - i for i, s in enumerate(source)} - {0}):
        hit = None
        for i, s in enumerate(source):
            if s - i == move:
                hit = (site.by == i) if hit is None else hit | (site.by == i)
        out = jnp.where(hit, left(x, move), out)
    return out


SPLIT_Y = (0, 2, 4, 6, 1, 3, 5, 7)
JOIN_Y = (0, 4, 1, 5, 2, 6, 3, 7)


def total_rows(x):
    for d in (4, 2, 1):
        x = x + up(x, d)
    return x


def widen(site, v):
    own = ((site.lane >> 3) & 7) == site.row
    half = site.lane_bit(64) == site.lane_bit(8)
    found = []

    def down(x, d):
        if d == 8:
            x = jnp.where(half, x, flip_lane(site, x, 8))
            found.append(total_rows(jnp.where(own, x, 0.0)))
            return
        bit = site.lane_bit(d)
        r = left(x, d)
        down(jnp.where(bit, r, x), d // 2)
        down(jnp.where(bit, x, r), d // 2)

    for x in v:
        down(permute_eight(site, x, SPLIT_Y), 64)
    return found


def narrow(site, tiles):
    own = ((site.lane >> 3) & 7) == site.row
    same = site.lane_bit(64) == site.lane_bit(8)

    def fold(d, a, b):
        bit = site.lane_bit(d)
        return jnp.where(bit, b, a) + flip_lane(site, jnp.where(bit, a, b), d)

    out = []
    for q in range(0, 24, 8):
        t = [jnp.where(own, total_rows(x), 0.0) for x in tiles[q : q + 8]]
        t = [fold(8, t[i], t[i + 4]) for i in range(4)]
        t = [fold(32, t[i], t[i + 2]) for i in range(2)]
        x = fold(16, t[0], t[1])
        x = jnp.where(same, x, jnp.where(site.lane_bit(64), left(x, -56), left(x, 56)))
        out.append(permute_eight(site, x, JOIN_Y))
    return out


def restrict_mid(site, near_ref, v, tile_ref):
    x = widen(site, v)
    x_im = x[12:] + [-t for t in x[:12]]
    for o in range(0, 48, 16):
        re = [None, None]
        im = [None, None]
        for j in range(24):
            n = near_ref[pl.ds(o, 16), pl.ds(128 * j, 128)].astype(F32)
            for h in range(2):
                block = n[8 * h : 8 * h + 8]
                a, b = block * x[j], block * x_im[j]
                re[h] = a if re[h] is None else re[h] + a
                im[h] = b if im[h] is None else im[h] + b
        for h in range(2):
            tile_ref[0, pl.ds(o + 8 * h, 8), :] = re[h]
            tile_ref[1, pl.ds(o + 8 * h, 8), :] = im[h]
    dims = (((1,), (1,)), ((), ()))
    z = None
    for p in range(2):
        t = lax.dot_general(pick_y(p), tile_ref[p], dims, precision=HIGHEST, preferred_element_type=F32)
        z = t if z is None else z + t
    return z


def prolong_mid(site, near_ref, y3, row_ref):
    dims = (((0,), (0,)), ((), ()))
    for p in range(2):
        row_ref[p] = lax.dot_general(y3, pick_y(p), dims, precision=HIGHEST, preferred_element_type=F32)
    a, b = [None] * 24, [None] * 24
    for j in range(24):
        for o in range(0, 48, 16):
            n = near_ref[pl.ds(o, 16), pl.ds(128 * j, 128)].astype(F32)
            for h in range(2):
                block = n[8 * h : 8 * h + 8]
                s = block * row_ref[0, pl.ds(o + 8 * h, 8), :]
                t = block * row_ref[1, pl.ds(o + 8 * h, 8), :]
                a[j] = s if a[j] is None else a[j] + s
                b[j] = t if b[j] is None else b[j] + t
    tiles = [a[j] - b[12 + j] for j in range(12)] + [a[12 + j] + b[j] for j in range(12)]
    return narrow(site, tiles)


def coarse_rows(v):
    high = v.astype(BF16).astype(F32)
    return jnp.concatenate([high, v - high], axis=0).astype(BF16)


def coarse_matrix(terms):
    row = iota2((8, 48), 0)
    total = None
    for ref, base, v in terms:
        turned = jnp.where(row < 4, -up(v, 4), up(v, 4))
        for a, x in enumerate((v, turned)):
            t = jnp.dot(coarse_rows(x), ref[pl.ds(base + 48 * a, 48), :], preferred_element_type=F32)
            total = t if total is None else total + t
    both = total[:8] + total[8:]
    out = None
    for y in range(4):
        t = jnp.where((row & 3) == y, both[:, 48 * y : 48 * y + 48], 0.0)
        out = t if out is None else out + t
    return out


def coarse_stencil_apply(ref, v, ahead, behind):
    y = iota2((8, 48), 0) & 3
    shifted = [v]
    for direction in range(3):
        shifted += [ahead[direction], behind[direction]]
    shifted.append(jnp.where(y == 3, up(v, -3), up(v, 1)))
    shifted.append(jnp.where(y == 0, up(v, 3), up(v, -1)))
    return coarse_matrix([(ref, 96 * k, s) for k, s in enumerate(shifted)])


def load(ref, n, base=0):
    return [ref[base + i] for i in range(n)]


def store(ref, values, base=0):
    for i, x in enumerate(values):
        ref[base + i] = x


def is_odd(axis):
    return lax.rem(lax.axis_index(axis), 2) == 1


def finish_fine(site, links_ref, solution, sol_ref, acc_ref, z0_ref, z1_ref, t0_ref, t1_ref):
    store(sol_ref, solution)
    back_t, back_z = fine_send(site, links_ref, solution, acc_ref)
    for axis, back, ref0, ref1 in (("gz", back_z, z0_ref, z1_ref), ("ta", back_t, t0_ref, t1_ref)):
        odd = is_odd(axis)
        store(ref0, [jnp.where(odd, s, b) for s, b in zip(solution, back)])
        store(ref1, [jnp.where(odd, b, s) for s, b in zip(solution, back)])


def by_parity(axis, zero, one):
    odd = is_odd(axis)
    ahead = [jnp.where(odd, b, a) for a, b in zip(zero, one)]
    return ahead, [jnp.where(odd, a, b) for a, b in zip(zero, one)]


def begin_fine(site, links_ref, refs):
    sol_ref, acc_ref, t0, z1, z0, t1, x, gx_ref = refs
    solution = load(sol_ref, 6)
    ahead_t, behind_t = by_parity("ta", load(t0, 6), load(t1, 6))
    ahead_z, behind_z = by_parity("gz", load(z0, 6), load(z1, 6))
    ahead = [ahead_t, ahead_z, load(x, 6)]
    near, far = backward(site, PairedLinks(gx_ref), ahead[2], 2)
    first = site.first(2)
    behind = [behind_t, behind_z, [jnp.where(first, n, f) for n, f in zip(near, far)]]
    return solution, fine_receive(site, links_ref, solution, load(acc_ref, 6), ahead, behind)


def row_order(transposed):
    m, n = iota2((64, 64), 0), iota2((64, 64), 1)
    if transposed:
        m, n = n, m
    bit = lambda v, k: (v >> k) & 1
    fine = (
        (bit(m, 2) << 5) | (bit(m, 5) << 4) | (bit(m, 1) << 3) | (bit(m, 4) << 2) | (bit(m, 0) << 1) | bit(m, 3)
    )
    return n == fine


def y_order(rows, columns, transposed):
    m, n = iota2((rows, columns), 0), iota2((rows, columns), 1)
    if transposed:
        m, n = n, m
    fine = (((n & 7) << 1) | ((n >> 3) & 1)) | (n & 112)
    return (m == (fine & (min(rows, columns) - 1))).astype(BF16)


def dot(a, b):
    return jnp.dot(a, b, preferred_element_type=F32)


def three_parts(x):
    high = x.astype(BF16)
    rest = x - high.astype(F32)
    mid = rest.astype(BF16)
    return high, mid, (rest - mid.astype(F32)).astype(BF16)


def prepare_links(site, links_ref, g_ref, gx_ref):
    rows = row_order(False).astype(BF16)
    lanes = y_order(128, 128, False)
    signs = [jnp.full((8, 128), 0.5, F32)]
    for d in LANE_BITS:
        signs.append(jnp.where(site.lane_bit(d), -signs[-1], signs[-1]))
    for rc in range(9):
        parts = [links_ref[rc // 3, rc % 3, t, z].astype(F32) for t in range(4) for z in range(4)]
        block = dot(rows, jnp.concatenate(parts, axis=0).astype(BF16)).astype(BF16)
        for h in range(2):
            half = dot(block[:, 128 * h : 128 * h + 128], lanes)
            v = [half[8 * w : 8 * w + 8] for w in range(8)]
            for d, k in zip(LANE_BITS, (4, 2, 1)):
                bit = site.lane_bit(d)
                for w in range(8):
                    if not w & k:
                        lo, hi = v[w], v[w | k]
                        v[w] = jnp.where(bit, left(hi, -d), lo)
                        v[w | k] = jnp.where(bit, hi, left(lo, d))
            for m in range(8):
                g_ref[(8 * h + m) * 9 + rc] = v[m] * signs[2 * h + m // 4]
    for i in range(0, 36, 2):
        gx_ref[i // 2] = jnp.concatenate([g_ref[72 + i], g_ref[73 + i]], axis=0).astype(BF16)


def gather_fine(site, field_ref):
    rows = row_order(False).astype(BF16)
    lanes = y_order(16, 128, False)
    group = site.lane >> 4
    out = []
    for p in range(2):
        for c in range(3):
            parts = [field_ref[p, c, t, z] for t in range(4) for z in range(4)]
            moved = [dot(rows, x) for x in three_parts(jnp.concatenate(parts, axis=0))]
            wide = dot(jnp.concatenate(moved, axis=0).astype(BF16), lanes)
            total = None
            for w in range(8):
                own = wide[8 * w : 8 * w + 8] + wide[64 + 8 * w : 72 + 8 * w] + wide[128 + 8 * w : 136 + 8 * w]
                total = own if w == 0 else jnp.where(group == w, own, total)
            out.append(total)
    return out


def scatter_fine(site, field, out_ref):
    rows = row_order(True).astype(F32)
    rows = jnp.concatenate([rows, rows, rows], axis=1).astype(BF16)
    lanes = y_order(128, 16, True)
    group = site.lane >> 4
    for p in range(2):
        for c in range(3):
            parts = [x.astype(F32) for x in three_parts(field[3 * p + c])]
            tall = jnp.concatenate([jnp.where(group == w, x, 0.0) for x in parts for w in range(8)], axis=0)
            value = dot(rows, dot(tall.astype(BF16), lanes).astype(BF16))
            for t in range(4):
                for z in range(4):
                    out_ref[p, c, t, z] = value[16 * t + 4 * z : 16 * t + 4 * z + 4]


def kernel_links(block_ref, links_ref, g_ref, gx_ref):
    prepare_links(Site(), links_ref, g_ref, gx_ref)


def kernel_first(g_ref, block_ref, source_ref, rhs_ref, *outs):
    site = Site()
    rhs = gather_fine(site, source_ref)
    store(rhs_ref, rhs)
    finish_fine(site, g_ref, fine_matrix(site, block_ref, rhs), *outs)


def kernel_smooth(links_ref, block_ref, rhs_ref, *refs):
    site = Site()
    solution, applied = begin_fine(site, links_ref, refs[:8])
    residual = sub(load(rhs_ref, 6), applied)
    solution = add(solution, fine_matrix(site, block_ref, residual))
    finish_fine(site, links_ref, solution, *refs[8:])


def kernel_last(links_ref, rhs_ref, *refs):
    site = Site()
    _, applied = begin_fine(site, links_ref, refs[:8])
    scatter_fine(site, sub(load(rhs_ref, 6), applied), refs[8])


def kernel_scatter(field_ref, out_ref):
    scatter_fine(Site(), load(field_ref, 6), out_ref)


def kernel_restrict(links_ref, near_ref, jacobi_ref, rhs_ref, *refs):
    site = Site()
    _, applied = begin_fine(site, links_ref, refs[:8])
    residual = sub(load(rhs_ref, 6), applied)
    mid_res = restrict_fine(site, near_ref, residual)
    store(refs[8], mid_res)
    store(refs[9], mid_matrix(site, jacobi_ref, mid_res))


def neighbours(refs, get):
    nx, t1, z0, z1, t0 = refs
    ahead_t, behind_t = by_parity("ta", get(t0), get(t1))
    ahead_z, behind_z = by_parity("gz", get(z0), get(z1))
    return [ahead_t, ahead_z, get(nx)], [behind_t, behind_z, get(nx)]


def kernel_mid_down(stencil_ref, near_ref, jacobi_ref, res_ref, sol_ref, *refs):
    site = Site()
    around, (r3_ref, y3_ref, tile_ref) = refs[:-3], refs[-3:]
    ahead, behind = neighbours(around, lambda r: load(r, 3))
    applied = mid_stencil_apply(site, stencil_ref, load(sol_ref, 3), ahead, behind)
    r3 = restrict_mid(site, near_ref, sub(load(res_ref, 3), applied), tile_ref)
    r3_ref[...] = r3
    y3_ref[...] = coarse_matrix([(jacobi_ref, 0, r3)])


def sweep(stencil_ref, jacobi_ref, r3_ref, y3_ref, around):
    ahead, behind = neighbours(around, lambda r: [r[...]])
    ahead, behind = [x[0] for x in ahead], [x[0] for x in behind]
    y3 = y3_ref[...]
    rest = r3_ref[...] - coarse_stencil_apply(stencil_ref, y3, ahead, behind)
    return y3 + coarse_matrix([(jacobi_ref, 0, rest)])


def kernel_sweep(stencil_ref, jacobi_ref, r3_ref, y3_ref, *refs):
    refs[-1][...] = sweep(stencil_ref, jacobi_ref, r3_ref, y3_ref, refs[:-1])


def kernel_sweep_up(stencil_ref, jacobi_ref, near_ref, y2_ref, r3_ref, y3_ref, *refs):
    site = Site()
    around, (out_ref, row_ref) = refs[:-2], refs[-2:]
    y3 = sweep(stencil_ref, jacobi_ref, r3_ref, y3_ref, around)
    store(out_ref, add(load(y2_ref, 3), prolong_mid(site, near_ref, y3, row_ref)))


def kernel_mid_up(links_ref, stencil_ref, jacobi_ref, near_ref, old_ref, res_ref, y2_ref, *refs):
    site = Site()
    around, outs, spread_ref = refs[:-7], refs[-7:-1], refs[-1]
    ahead, behind = neighbours(around, lambda r: load(r, 3))
    y2 = load(y2_ref, 3)
    rest = sub(load(res_ref, 3), mid_stencil_apply(site, stencil_ref, y2, ahead, behind))
    y2 = add(y2, mid_matrix(site, jacobi_ref, rest))
    solution = add(load(old_ref, 6), prolong_fine(site, near_ref, y2, spread_ref))
    finish_fine(site, links_ref, solution, *outs)


def call(kernel, outs, scratch, *args, first_any=False):
    specs = [pl.BlockSpec(memory_space=pltpu.VMEM)] * len(args)
    if first_any:
        specs[0] = pl.BlockSpec(memory_space=pl.ANY)
    return pl.pallas_call(
        kernel,
        out_shape=[jax.ShapeDtypeStruct(*s) if s[1] == BF16 else jax.ShapeDtypeStruct(s, F32) for s in outs],
        in_specs=specs,
        scratch_shapes=[pltpu.VMEM(s, F32) for s in scratch],
        compiler_params=pltpu.CompilerParams(vmem_limit_bytes=VMEM_BYTES),
        name=kernel.__name__,
    )(*args)


def from_behind(block, axis, distance):
    n = lax.axis_size(axis)
    return lax.ppermute(block, axis, [((i - distance) % n, i) for i in range(n)])


def swap(block, axis, phase):
    n = lax.axis_size(axis)
    return lax.ppermute(block, axis, [(i, (((i + phase) ^ 1) - phase) % n) for i in range(n)])


def exchange(v):
    x = from_behind(v, "xy", 1)
    t1 = swap(v, "ta", 1)
    z0 = swap(v, "gz", 0)
    z1 = swap(v, "gz", 1)
    return [x, t1, z0, z1, swap(v, "ta", 0)]


def exchange_fine(gx, sol, acc, z0, z1, t0, t1):
    x = from_behind(sol, "xy", 1)
    t1 = swap(t1, "ta", 1)
    z0 = swap(z0, "gz", 0)
    z1 = swap(z1, "gz", 1)
    t0 = swap(t0, "ta", 0)
    return [sol, acc, t0, z1, z0, t1, x, gx]


TILE6 = (6, 8, 128)
FINE_OUT = [TILE6] * 6


def local(
    right_side,
    links,
    block_inverse,
    near_fine,
    mid_stencil,
    mid_jacobi,
    near_mid,
    coarse_stencil,
    coarse_jacobi,
):
    block = block_inverse.reshape(384, 768)
    near1 = near_fine.reshape(192, 768)
    stencil2 = mid_stencil.reshape(1728, 384)
    jacobi2 = mid_jacobi.reshape(192, 384)
    near2 = near_mid.reshape(near_mid.shape[0], near_mid.shape[4])
    stencil3 = jnp.swapaxes(coarse_stencil, 5, 6).reshape(864, 192)
    jacobi3 = jnp.swapaxes(coarse_jacobi, 4, 5).reshape(96, 192)
    mid = (3, 8, 128)
    coarse = (8, 48)

    g, gx = call(kernel_links, [(144, 8, 128), ((18, 16, 128), BF16)], [], block, links, first_any=True)
    gx = from_behind(gx, "xy", 1)
    rhs, *state = call(kernel_first, [TILE6] + FINE_OUT, [], g, block, right_side)
    for cycle_no in range(CYCLES):
        r2, y2 = call(kernel_restrict, [mid, mid], [], g, near1, jacobi2, rhs, *exchange_fine(gx, *state))
        r3, y3 = call(
            kernel_mid_down, [coarse, coarse], [(2, 48, 128)], stencil2, near2, jacobi3, r2, y2, *exchange(y2)
        )
        for _ in range(SWEEPS - 1):
            (y3,) = call(kernel_sweep, [coarse], [], stencil3, jacobi3, r3, y3, *exchange(y3))
        (y2,) = call(
            kernel_sweep_up, [mid], [(2, 48, 128)], stencil3, jacobi3, near2, y2, r3, y3, *exchange(y3)
        )
        state = call(
            kernel_mid_up, FINE_OUT, [(48, 8, 128)], g, stencil2, jacobi2, near1, state[0], r2, y2, *exchange(y2)
        )
        state = call(kernel_smooth, FINE_OUT, [], g, block, rhs, *exchange_fine(gx, *state))
        if cycle_no < CYCLES - 1:
            state = call(kernel_smooth, FINE_OUT, [], g, block, rhs, *exchange_fine(gx, *state))
    around = exchange_fine(gx, *state)
    (solution,) = call(kernel_scatter, [right_side.shape], [], state[0])
    (residual,) = call(kernel_last, [right_side.shape], [], g, rhs, *around)
    return solution, residual


def solution(mesh):
    return jax.shard_map(
        local,
        mesh=mesh,
        in_specs=(
            P(None, None, "ta", "gz", "xy", None),
            P(None, None, "ta", "gz", "xy", None),
            P(None, "ta", "gz", "xy", None),
            P(None, "ta", "gz", "xy", None),
            P(None, None, "ta", "gz", "xy", None),
            P(None, "ta", "gz", "xy", None),
            P(None, "ta", "gz", "xy", None),
            P(None, None, "ta", "gz", "xy", None, None),
            P(None, "ta", "gz", "xy", None, None),
        ),
        out_specs=(P(None, None, "ta", "gz", "xy", None), P(None, None, "ta", "gz", "xy", None)),
        check_vma=False,
    )
```

```python
import jax
import jax.numpy as jnp
from jax import lax
from jax.sharding import PartitionSpec as P
import jax.experimental.pallas as pl
from jax.experimental.pallas import tpu as pltpu

SWEEPS = 4
CYCLES = 2
F32 = jnp.float32
BF16 = jnp.bfloat16
HIGHEST = lax.Precision.HIGHEST
LANE_BITS = (64, 32, 16)
ROW_BITS = (4, 2, 1)
VMEM_BYTES = 24 << 20


class Site:
    def __init__(self):
        self.lane = lax.broadcasted_iota(jnp.int32, (8, 128), 1)
        self.row = lax.broadcasted_iota(jnp.int32, (8, 128), 0)
        self.by = self.lane & 7

    def lane_bit(self, d):
        return (self.lane & d) != 0

    def row_bit(self, d):
        return (self.row & d) != 0

    def first(self, direction):
        return ((self.lane & LANE_BITS[direction]) | (self.row & ROW_BITS[direction])) == 0

    def last(self, direction):
        return self.lane_bit(LANE_BITS[direction]) & self.row_bit(ROW_BITS[direction])


def left(x, s):
    s = s % 128
    return pltpu.roll(x, (128 - s) % 128, 1) if s else x


def up(x, s):
    s = s % 8
    return pltpu.roll(x, (8 - s) % 8, 0) if s else x


def flip_lane(site, x, d):
    if d == 64:
        return left(x, 64)
    return jnp.where(site.lane_bit(d), left(x, -d), left(x, d))


def flip_row(site, x, d):
    if d == 4:
        return up(x, 4)
    return jnp.where(site.row_bit(d), up(x, -d), up(x, d))


def cyclic(site, x, direction, sign):
    d = LANE_BITS[direction]
    flipped = flip_lane(site, x, d)
    both = flip_row(site, flipped, ROW_BITS[direction])
    if sign > 0:
        return jnp.where(site.lane_bit(d), both, flipped)
    return jnp.where(site.lane_bit(d), flipped, both)


def by_roll(site, x, base, q):
    moved = left(x, base + q)
    if q == 0:
        return moved
    if q > 0:
        return jnp.where(site.by >= 8 - q, left(x, base + q - 8), moved)
    return jnp.where(site.by < -q, left(x, base + q + 8), moved)


def shift_y(site, x, n):
    found = []
    for c in (0, 1):
        c_new = (c + n) % 2
        q = (c + n - c_new) // 2
        found.append(by_roll(site, x, 8 * (c_new - c), q))
    return jnp.where(site.lane_bit(8), found[1], found[0])


def link(links_ref, mu, kind, part, r, c):
    return links_ref[((mu * 2 + kind) * 2 + part) * 9 + r * 3 + c]


def link_apply(links_ref, mu, kind, field):
    out = [None] * 6
    for r in range(3):
        re = im = None
        for c in range(3):
            g_re = link(links_ref, mu, kind, 0, r, c)
            g_im = link(links_ref, mu, kind, 1, r, c)
            a = g_re * field[c] - g_im * field[3 + c]
            b = g_re * field[3 + c] + g_im * field[c]
            re = a if re is None else re + a
            im = b if im is None else im + b
        out[r] = re
        out[3 + r] = im
    return out


def link_adjoint(links_ref, mu, kind, field):
    out = [None] * 6
    for c in range(3):
        re = im = None
        for r in range(3):
            g_re = link(links_ref, mu, kind, 0, r, c)
            g_im = link(links_ref, mu, kind, 1, r, c)
            a = g_re * field[r] + g_im * field[3 + r]
            b = g_re * field[3 + r] - g_im * field[r]
            re = a if re is None else re + a
            im = b if im is None else im + b
        out[c] = re
        out[3 + c] = im
    return out


def add(xs, ys):
    return [x + y for x, y in zip(xs, ys)]


def sub(xs, ys):
    return [x - y for x, y in zip(xs, ys)]


def fine_send(site, links_ref, field):
    sent = []
    for direction in range(2):
        near, far = backward(site, links_ref, field, direction)
        first = site.first(direction)
        sent.append([jnp.where(first, n, f) for n, f in zip(near, far)])
    return sent


def fine_own(site, links_ref, field):
    acc = list(field)
    for kind, reach in ((0, 1), (1, 3)):
        acc = add(acc, link_apply(links_ref, 3, kind, [shift_y(site, x, reach) for x in field]))
        back = link_adjoint(links_ref, 3, kind, field)
        acc = sub(acc, [shift_y(site, x, -reach) for x in back])
    for direction in range(3):
        near, far = backward(site, links_ref, field, direction)
        first, last = site.first(direction), site.last(direction)
        acc = [
            a - jnp.where(first, 0.0, n) - jnp.where(last, cyclic(site, f, direction, 1), 0.0)
            for a, n, f in zip(acc, near, far)
        ]
    return acc


class PairedLinks:
    def __init__(self, ref):
        self.ref = ref

    def __getitem__(self, i):
        i -= 72
        return self.ref[i // 2].astype(F32)[8 * (i % 2) : 8 * (i % 2) + 8]


def backward(site, links_ref, field, direction):
    near = [cyclic(site, x, direction, -1) for x in link_adjoint(links_ref, direction, 0, field)]
    return near, link_adjoint(links_ref, direction, 1, field)


def fine_receive(site, links_ref, field, acc, ahead, behind):
    out = acc
    for direction in range(3):
        first, last = site.first(direction), site.last(direction)
        nxt = ahead[direction]
        one = [cyclic(site, jnp.where(first, n, x), direction, 1) for n, x in zip(nxt, field)]
        out = add(out, link_apply(links_ref, direction, 0, one))
        three = [cyclic(site, jnp.where(last, x, n), direction, -1) for n, x in zip(nxt, field)]
        out = add(out, link_apply(links_ref, direction, 1, three))
        out = [
            o - jnp.where(first, b, 0.0) - jnp.where(last, 0.0, cyclic(site, b, direction, 1))
            for o, b in zip(out, behind[direction])
        ]
    return out


def merge(site, d, a, b):
    bit = site.lane_bit(d)
    return jnp.where(bit, b, a) + left(jnp.where(bit, a, b), d)


def tree(site, leaf, base, n):
    if n == 2:
        a, b = leaf(base)
    else:
        a = tree(site, leaf, base, n // 2)
        b = tree(site, leaf, base + n // 2, n // 2)
    return [merge(site, 4 * n, x, y) for x, y in zip(a, b)]


def two_rows(ref, o):
    return ref[pl.ds(o * 8, 16), :].astype(F32)


def dot_tiles(block, row, x):
    total = None
    for j, v in enumerate(x):
        term = block[row : row + 8, 128 * j : 128 * j + 128] * v
        total = term if total is None else total + term
    return total


def pair_leaf(terms):
    def leaf(o):
        sums = [[None, None], [None, None]]
        for ref, base, x_re, x_im in terms:
            block = two_rows(ref, base + o)
            for h in range(2):
                for p, x in enumerate((x_re, x_im)):
                    t = dot_tiles(block, 8 * h, x)
                    sums[h][p] = t if sums[h][p] is None else sums[h][p] + t
        return sums

    return leaf


def fine_matrix(site, ref, field):
    x_re = field[:3] + [-x for x in field[3:]]
    x_im = field[3:] + field[:3]
    out = [tree(site, pair_leaf([(ref, 0, x_re, x_im)]), 16 * c, 16) for c in range(3)]
    return [o[0] for o in out] + [o[1] for o in out]


def mid_gather(site, terms):
    leaf = pair_leaf(terms)
    eight = [tree(site, leaf, 8 * j, 8) for j in range(3)]
    return [
        merge(site, 64, eight[0][0], eight[1][0]),
        merge(site, 64, eight[2][0], eight[0][1]),
        merge(site, 64, eight[1][1], eight[2][1]),
    ]


def swap_parts(site, v):
    low = jnp.logical_not(site.lane_bit(64))
    r = [left(x, 64) for x in v]
    return [jnp.where(low, r[1], r[2]), jnp.where(low, r[2], r[0]), jnp.where(low, r[0], r[1])]


def im_negated(site, v):
    return [v[0], jnp.where(site.lane_bit(64), -v[1], v[1]), -v[2]]


def mid_x(site, v):
    return im_negated(site, v), swap_parts(site, v)


def mid_x_conj(site, v):
    return v, im_negated(site, swap_parts(site, v))


def restrict_fine(site, near_ref, field):
    x_im = field[3:] + [-x for x in field[:3]]
    return mid_gather(site, [(near_ref, 0, field, x_im)])


def mid_matrix(site, ref, v):
    x_re, x_im = mid_x(site, v)
    return mid_gather(site, [(ref, 0, x_re, x_im)])


def mid_stencil_own(site, ref, v):
    shifted = ((0, v), (7, [by_roll(site, x, 0, 1) for x in v]), (8, [by_roll(site, x, 0, -1) for x in v]))
    return mid_gather(site, [(ref, 24 * k) + mid_x(site, s) for k, s in shifted])


def mid_stencil_near(site, ref, v, ahead, behind):
    shifted = []
    for direction in range(3):
        d = ROW_BITS[direction]
        bit = site.row_bit(d)
        shifted.append([flip_row(site, jnp.where(bit, x, n), d) for x, n in zip(v, ahead[direction])])
        shifted.append([flip_row(site, jnp.where(bit, n, x), d) for x, n in zip(v, behind[direction])])
    return mid_gather(site, [(ref, 24 * k + 24) + mid_x(site, s) for k, s in enumerate(shifted)])


def spread(site, v, ref):
    def down(x, base, d):
        if d == 4:
            ref[base] = x
            return
        bit = site.lane_bit(d)
        r = left(x, d)
        down(jnp.where(bit, r, x), base, d // 2)
        down(jnp.where(bit, x, r), base + d // 8, d // 2)

    for j, x in enumerate(v):
        down(x, 16 * j, 64)


def prolong_fine(site, near_ref, v, spread_ref):
    spread(site, v, spread_ref)
    a, b = [0.0] * 6, [0.0] * 6
    for o in range(0, 24, 2):
        block = two_rows(near_ref, o)
        for h in range(2):
            y_re, y_im = spread_ref[o + h], spread_ref[24 + o + h]
            for j in range(6):
                n = block[8 * h : 8 * h + 8, 128 * j : 128 * j + 128]
                a[j] = a[j] + n * y_re
                b[j] = b[j] + n * y_im
    return [a[j] - b[3 + j] for j in range(3)] + [a[3 + j] + b[j] for j in range(3)]


def iota2(shape, axis):
    return lax.broadcasted_iota(jnp.int32, shape, axis)


def pick_y(part):
    row, lane = iota2((8, 128), 0), iota2((8, 128), 1)
    return (row == part * 4 + (lane & 3)).astype(F32)


def permute_eight(site, x, source):
    out = x
    for move in sorted({s - i for i, s in enumerate(source)} - {0}):
        hit = None
        for i, s in enumerate(source):
            if s - i == move:
                hit = (site.by == i) if hit is None else hit | (site.by == i)
        out = jnp.where(hit, left(x, move), out)
    return out


SPLIT_Y = (0, 2, 4, 6, 1, 3, 5, 7)
JOIN_Y = (0, 4, 1, 5, 2, 6, 3, 7)


def total_rows(x):
    for d in (4, 2, 1):
        x = x + up(x, d)
    return x


def widen(site, v):
    own = ((site.lane >> 3) & 7) == site.row
    half = site.lane_bit(64) == site.lane_bit(8)
    found = []

    def down(x, d):
        if d == 8:
            x = jnp.where(half, x, flip_lane(site, x, 8))
            found.append(total_rows(jnp.where(own, x, 0.0)))
            return
        bit = site.lane_bit(d)
        r = left(x, d)
        down(jnp.where(bit, r, x), d // 2)
        down(jnp.where(bit, x, r), d // 2)

    for x in v:
        down(permute_eight(site, x, SPLIT_Y), 64)
    return found


def narrow(site, tiles):
    own = ((site.lane >> 3) & 7) == site.row
    same = site.lane_bit(64) == site.lane_bit(8)

    def fold(d, a, b):
        bit = site.lane_bit(d)
        return jnp.where(bit, b, a) + flip_lane(site, jnp.where(bit, a, b), d)

    out = []
    for q in range(0, 24, 8):
        t = [jnp.where(own, total_rows(x), 0.0) for x in tiles[q : q + 8]]
        t = [fold(8, t[i], t[i + 4]) for i in range(4)]
        t = [fold(32, t[i], t[i + 2]) for i in range(2)]
        x = fold(16, t[0], t[1])
        x = jnp.where(same, x, jnp.where(site.lane_bit(64), left(x, -56), left(x, 56)))
        out.append(permute_eight(site, x, JOIN_Y))
    return out


def restrict_mid(site, near_ref, v, tile_ref):
    x = widen(site, v)
    x_im = x[12:] + [-t for t in x[:12]]
    for o in range(0, 48, 16):
        re = [None, None]
        im = [None, None]
        for j in range(24):
            n = near_ref[pl.ds(o, 16), pl.ds(128 * j, 128)].astype(F32)
            for h in range(2):
                block = n[8 * h : 8 * h + 8]
                a, b = block * x[j], block * x_im[j]
                re[h] = a if re[h] is None else re[h] + a
                im[h] = b if im[h] is None else im[h] + b
        for h in range(2):
            tile_ref[0, pl.ds(o + 8 * h, 8), :] = re[h]
            tile_ref[1, pl.ds(o + 8 * h, 8), :] = im[h]
    dims = (((1,), (1,)), ((), ()))
    z = None
    for p in range(2):
        t = lax.dot_general(pick_y(p), tile_ref[p], dims, precision=HIGHEST, preferred_element_type=F32)
        z = t if z is None else z + t
    return z


def prolong_mid(site, near_ref, y3, row_ref):
    dims = (((0,), (0,)), ((), ()))
    for p in range(2):
        row_ref[p] = lax.dot_general(y3, pick_y(p), dims, precision=HIGHEST, preferred_element_type=F32)
    a, b = [None] * 24, [None] * 24
    for j in range(24):
        for o in range(0, 48, 16):
            n = near_ref[pl.ds(o, 16), pl.ds(128 * j, 128)].astype(F32)
            for h in range(2):
                block = n[8 * h : 8 * h + 8]
                s = block * row_ref[0, pl.ds(o + 8 * h, 8), :]
                t = block * row_ref[1, pl.ds(o + 8 * h, 8), :]
                a[j] = s if a[j] is None else a[j] + s
                b[j] = t if b[j] is None else b[j] + t
    tiles = [a[j] - b[12 + j] for j in range(12)] + [a[12 + j] + b[j] for j in range(12)]
    return narrow(site, tiles)


def coarse_rows(v):
    high = v.astype(BF16).astype(F32)
    return jnp.concatenate([high, v - high], axis=0).astype(BF16)


def coarse_matrix(terms):
    row = iota2((8, 48), 0)
    total = None
    for ref, base, v in terms:
        turned = jnp.where(row < 4, -up(v, 4), up(v, 4))
        for a, x in enumerate((v, turned)):
            t = jnp.dot(coarse_rows(x), ref[pl.ds(base + 48 * a, 48), :], preferred_element_type=F32)
            total = t if total is None else total + t
    both = total[:8] + total[8:]
    out = None
    for y in range(4):
        t = jnp.where((row & 3) == y, both[:, 48 * y : 48 * y + 48], 0.0)
        out = t if out is None else out + t
    return out


def coarse_stencil_own(ref, v):
    y = iota2((8, 48), 0) & 3
    up_y = jnp.where(y == 3, up(v, -3), up(v, 1))
    down_y = jnp.where(y == 0, up(v, 3), up(v, -1))
    return coarse_matrix([(ref, 0, v), (ref, 96 * 7, up_y), (ref, 96 * 8, down_y)])


def coarse_stencil_near(ref, ahead, behind):
    terms = []
    for direction in range(3):
        terms.append((ref, 96 * (2 * direction + 1), ahead[direction]))
        terms.append((ref, 96 * (2 * direction + 2), behind[direction]))
    return coarse_matrix(terms)


def load(ref, n, base=0):
    return [ref[base + i] for i in range(n)]


def store(ref, values, base=0):
    for i, x in enumerate(values):
        ref[base + i] = x


def is_odd(axis):
    return lax.rem(lax.axis_index(axis), 2) == 1


def finish_fine(site, links_ref, solution, sol_ref, z0_ref, z1_ref, t0_ref, t1_ref):
    store(sol_ref, solution)
    back_t, back_z = fine_send(site, links_ref, solution)
    for axis, back, ref0, ref1 in (("gz", back_z, z0_ref, z1_ref), ("ta", back_t, t0_ref, t1_ref)):
        odd = is_odd(axis)
        store(ref0, [jnp.where(odd, s, b) for s, b in zip(solution, back)])
        store(ref1, [jnp.where(odd, b, s) for s, b in zip(solution, back)])


def by_parity(axis, zero, one):
    odd = is_odd(axis)
    ahead = [jnp.where(odd, b, a) for a, b in zip(zero, one)]
    return ahead, [jnp.where(odd, a, b) for a, b in zip(zero, one)]


def begin_fine(site, links_ref, refs):
    sol_ref, acc_ref, t0, z1, z0, t1, x, gx_ref = refs
    solution = load(sol_ref, 6)
    ahead_t, behind_t = by_parity("ta", load(t0, 6), load(t1, 6))
    ahead_z, behind_z = by_parity("gz", load(z0, 6), load(z1, 6))
    ahead = [ahead_t, ahead_z, load(x, 6)]
    near, far = backward(site, PairedLinks(gx_ref), ahead[2], 2)
    first = site.first(2)
    behind = [behind_t, behind_z, [jnp.where(first, n, f) for n, f in zip(near, far)]]
    return solution, fine_receive(site, links_ref, solution, load(acc_ref, 6), ahead, behind)


def row_order(transposed):
    m, n = iota2((64, 64), 0), iota2((64, 64), 1)
    if transposed:
        m, n = n, m
    bit = lambda v, k: (v >> k) & 1
    fine = (
        (bit(m, 2) << 5) | (bit(m, 5) << 4) | (bit(m, 1) << 3) | (bit(m, 4) << 2) | (bit(m, 0) << 1) | bit(m, 3)
    )
    return n == fine


def y_order(rows, columns, transposed):
    m, n = iota2((rows, columns), 0), iota2((rows, columns), 1)
    if transposed:
        m, n = n, m
    fine = (((n & 7) << 1) | ((n >> 3) & 1)) | (n & 112)
    return (m == (fine & (min(rows, columns) - 1))).astype(BF16)


def dot(a, b):
    return jnp.dot(a, b, preferred_element_type=F32)


def three_parts(x):
    high = x.astype(BF16)
    rest = x - high.astype(F32)
    mid = rest.astype(BF16)
    return high, mid, (rest - mid.astype(F32)).astype(BF16)


def prepare_links(site, links_ref, g_ref, gx_ref):
    rows = row_order(False).astype(BF16)
    lanes = y_order(128, 128, False)
    signs = [jnp.full((8, 128), 0.5, F32)]
    for d in LANE_BITS:
        signs.append(jnp.where(site.lane_bit(d), -signs[-1], signs[-1]))
    for rc in range(9):
        parts = [links_ref[rc // 3, rc % 3, t, z].astype(F32) for t in range(4) for z in range(4)]
        block = dot(rows, jnp.concatenate(parts, axis=0).astype(BF16)).astype(BF16)
        for h in range(2):
            half = dot(block[:, 128 * h : 128 * h + 128], lanes)
            v = [half[8 * w : 8 * w + 8] for w in range(8)]
            for d, k in zip(LANE_BITS, (4, 2, 1)):
                bit = site.lane_bit(d)
                for w in range(8):
                    if not w & k:
                        lo, hi = v[w], v[w | k]
                        v[w] = jnp.where(bit, left(hi, -d), lo)
                        v[w | k] = jnp.where(bit, hi, left(lo, d))
            for m in range(8):
                g_ref[(8 * h + m) * 9 + rc] = v[m] * signs[2 * h + m // 4]
    for i in range(0, 36, 2):
        gx_ref[i // 2] = jnp.concatenate([g_ref[72 + i], g_ref[73 + i]], axis=0).astype(BF16)


def gather_fine(site, field_ref):
    rows = row_order(False).astype(BF16)
    lanes = y_order(16, 128, False)
    group = site.lane >> 4
    out = []
    for p in range(2):
        for c in range(3):
            parts = [field_ref[p, c, t, z] for t in range(4) for z in range(4)]
            moved = [dot(rows, x) for x in three_parts(jnp.concatenate(parts, axis=0))]
            wide = dot(jnp.concatenate(moved, axis=0).astype(BF16), lanes)
            total = None
            for w in range(8):
                own = wide[8 * w : 8 * w + 8] + wide[64 + 8 * w : 72 + 8 * w] + wide[128 + 8 * w : 136 + 8 * w]
                total = own if w == 0 else jnp.where(group == w, own, total)
            out.append(total)
    return out


def scatter_fine(site, field, out_ref):
    rows = row_order(True).astype(F32)
    rows = jnp.concatenate([rows, rows, rows], axis=1).astype(BF16)
    lanes = y_order(128, 16, True)
    group = site.lane >> 4
    for p in range(2):
        for c in range(3):
            parts = [x.astype(F32) for x in three_parts(field[3 * p + c])]
            tall = jnp.concatenate([jnp.where(group == w, x, 0.0) for x in parts for w in range(8)], axis=0)
            value = dot(rows, dot(tall.astype(BF16), lanes).astype(BF16))
            for t in range(4):
                for z in range(4):
                    out_ref[p, c, t, z] = value[16 * t + 4 * z : 16 * t + 4 * z + 4]


def kernel_links(links_ref, g_ref, gx_ref):
    prepare_links(Site(), links_ref, g_ref, gx_ref)


def kernel_first(g_ref, block_ref, source_ref, rhs_ref, *outs):
    site = Site()
    rhs = gather_fine(site, source_ref)
    store(rhs_ref, rhs)
    finish_fine(site, g_ref, fine_matrix(site, block_ref, rhs), *outs)


def kernel_smooth(links_ref, block_ref, rhs_ref, *refs):
    site = Site()
    solution, applied = begin_fine(site, links_ref, refs[:8])
    residual = sub(load(rhs_ref, 6), applied)
    solution = add(solution, fine_matrix(site, block_ref, residual))
    finish_fine(site, links_ref, solution, *refs[8:])


def kernel_last(links_ref, rhs_ref, *refs):
    site = Site()
    _, applied = begin_fine(site, links_ref, refs[:8])
    scatter_fine(site, sub(load(rhs_ref, 6), applied), refs[8])


def kernel_own(links_ref, field_ref, acc_ref):
    store(acc_ref, fine_own(Site(), links_ref, load(field_ref, 6)))


def kernel_scatter(field_ref, out_ref):
    scatter_fine(Site(), load(field_ref, 6), out_ref)


def kernel_restrict(links_ref, near_ref, jacobi_ref, rhs_ref, *refs):
    site = Site()
    _, applied = begin_fine(site, links_ref, refs[:8])
    residual = sub(load(rhs_ref, 6), applied)
    mid_res = restrict_fine(site, near_ref, residual)
    store(refs[8], mid_res)
    store(refs[9], mid_matrix(site, jacobi_ref, mid_res))


def neighbours(refs, get):
    nx, t1, z0, z1, t0 = refs
    ahead_t, behind_t = by_parity("ta", get(t0), get(t1))
    ahead_z, behind_z = by_parity("gz", get(z0), get(z1))
    return [ahead_t, ahead_z, get(nx)], [behind_t, behind_z, get(nx)]


def kernel_mid_own(stencil_ref, v_ref, out_ref):
    site = Site()
    store(out_ref, mid_stencil_own(site, stencil_ref, load(v_ref, 3)))


def mid_rest(site, stencil_ref, res_ref, y2_ref, own_ref, around):
    ahead, behind = neighbours(around, lambda r: load(r, 3))
    applied = mid_stencil_near(site, stencil_ref, load(y2_ref, 3), ahead, behind)
    return sub(load(res_ref, 3), add(load(own_ref, 3), applied))


def kernel_mid_down(stencil_ref, near_ref, jacobi_ref, res_ref, y2_ref, own_ref, *refs):
    site = Site()
    around, (r3_ref, y3_ref, tile_ref) = refs[:-3], refs[-3:]
    rest = mid_rest(site, stencil_ref, res_ref, y2_ref, own_ref, around)
    r3 = restrict_mid(site, near_ref, rest, tile_ref)
    r3_ref[...] = r3
    y3_ref[...] = coarse_matrix([(jacobi_ref, 0, r3)])


def kernel_sweep_own(stencil_ref, r3_ref, y3_ref, out_ref):
    out_ref[...] = r3_ref[...] - coarse_stencil_own(stencil_ref, y3_ref[...])


def sweep(stencil_ref, jacobi_ref, own_ref, y3_ref, around):
    ahead, behind = neighbours(around, lambda r: [r[...]])
    ahead, behind = [x[0] for x in ahead], [x[0] for x in behind]
    rest = own_ref[...] - coarse_stencil_near(stencil_ref, ahead, behind)
    return y3_ref[...] + coarse_matrix([(jacobi_ref, 0, rest)])


def kernel_sweep(stencil_ref, jacobi_ref, own_ref, y3_ref, *refs):
    refs[-1][...] = sweep(stencil_ref, jacobi_ref, own_ref, y3_ref, refs[:-1])


def kernel_sweep_up(stencil_ref, jacobi_ref, near_ref, y2_ref, own_ref, y3_ref, *refs):
    site = Site()
    around, (out_ref, row_ref) = refs[:-2], refs[-2:]
    y3 = sweep(stencil_ref, jacobi_ref, own_ref, y3_ref, around)
    store(out_ref, add(load(y2_ref, 3), prolong_mid(site, near_ref, y3, row_ref)))


def kernel_mid_up(links_ref, stencil_ref, jacobi_ref, near_ref, old_ref, res_ref, y2_ref, own_ref, *refs):
    site = Site()
    around, outs, spread_ref = refs[:-6], refs[-6:-1], refs[-1]
    rest = mid_rest(site, stencil_ref, res_ref, y2_ref, own_ref, around)
    y2 = add(load(y2_ref, 3), mid_matrix(site, jacobi_ref, rest))
    solution = add(load(old_ref, 6), prolong_fine(site, near_ref, y2, spread_ref))
    finish_fine(site, links_ref, solution, *outs)


def call(kernel, outs, scratch, *args, after=()):
    def body(*refs):
        kernel(*refs[len(after) :])

    specs = [pl.BlockSpec(memory_space=pl.ANY)] * len(after)
    return pl.pallas_call(
        body,
        out_shape=[jax.ShapeDtypeStruct(*s) if s[1] == BF16 else jax.ShapeDtypeStruct(s, F32) for s in outs],
        in_specs=specs + [pl.BlockSpec(memory_space=pltpu.VMEM)] * len(args),
        scratch_shapes=[pltpu.VMEM(s, F32) for s in scratch],
        compiler_params=pltpu.CompilerParams(vmem_limit_bytes=VMEM_BYTES),
        name=kernel.__name__,
    )(*after, *args)


def from_behind(block, axis, distance):
    n = lax.axis_size(axis)
    return lax.ppermute(block, axis, [((i - distance) % n, i) for i in range(n)])


def swap(block, axis, phase):
    n = lax.axis_size(axis)
    return lax.ppermute(block, axis, [(i, (((i + phase) ^ 1) - phase) % n) for i in range(n)])


def exchange(v):
    x = from_behind(v, "xy", 1)
    t1 = swap(v, "ta", 1)
    z0 = swap(v, "gz", 0)
    z1 = swap(v, "gz", 1)
    t0 = swap(v, "ta", 0)
    return [x, t1, z0, z1, t0]


def exchange_fine(g, gx, sol, z0, z1, t0, t1):
    x = from_behind(sol, "xy", 1)
    t1 = swap(t1, "ta", 1)
    z0 = swap(z0, "gz", 0)
    z1 = swap(z1, "gz", 1)
    t0 = swap(t0, "ta", 0)
    (acc,) = call(kernel_own, [TILE6], [], g, sol)
    return [sol, acc, t0, z1, z0, t1, x, gx]


TILE6 = (6, 8, 128)
FINE_OUT = [TILE6] * 5


def local(
    right_side,
    links,
    block_inverse,
    near_fine,
    mid_stencil,
    mid_jacobi,
    near_mid,
    coarse_stencil,
    coarse_jacobi,
):
    block = block_inverse.reshape(384, 768)
    near1 = near_fine.reshape(192, 768)
    stencil2 = mid_stencil.reshape(1728, 384)
    jacobi2 = mid_jacobi.reshape(192, 384)
    near2 = near_mid.reshape(near_mid.shape[0], near_mid.shape[4])
    stencil3 = jnp.swapaxes(coarse_stencil, 5, 6).reshape(864, 192)
    jacobi3 = jnp.swapaxes(coarse_jacobi, 4, 5).reshape(96, 192)
    mid = (3, 8, 128)
    coarse = (8, 48)

    g, gx = call(kernel_links, [(144, 8, 128), ((18, 16, 128), BF16)], [], links, after=(block,))
    gx = from_behind(gx, "xy", 1)
    rhs, *state = call(kernel_first, [TILE6] + FINE_OUT, [], g, block, right_side)
    for cycle_no in range(CYCLES):
        around = exchange_fine(g, gx, *state)
        r2, y2 = call(kernel_restrict, [mid, mid], [], g, near1, jacobi2, rhs, *around)
        around = exchange(y2)
        (own,) = call(kernel_mid_own, [mid], [], stencil2, y2)
        r3, y3 = call(
            kernel_mid_down, [coarse, coarse], [(2, 48, 128)], stencil2, near2, jacobi3, r2, y2, own, *around
        )
        for _ in range(SWEEPS - 1):
            around = exchange(y3)
            (own,) = call(kernel_sweep_own, [coarse], [], stencil3, r3, y3)
            (y3,) = call(kernel_sweep, [coarse], [], stencil3, jacobi3, own, y3, *around)
        around = exchange(y3)
        (own,) = call(kernel_sweep_own, [coarse], [], stencil3, r3, y3)
        (y2,) = call(
            kernel_sweep_up, [mid], [(2, 48, 128)], stencil3, jacobi3, near2, y2, own, y3, *around
        )
        around = exchange(y2)
        (own,) = call(kernel_mid_own, [mid], [], stencil2, y2)
        state = call(
            kernel_mid_up,
            FINE_OUT,
            [(48, 8, 128)],
            g,
            stencil2,
            jacobi2,
            near1,
            state[0],
            r2,
            y2,
            own,
            *around,
        )
        state = call(kernel_smooth, FINE_OUT, [], g, block, rhs, *exchange_fine(g, gx, *state))
        if cycle_no < CYCLES - 1:
            state = call(kernel_smooth, FINE_OUT, [], g, block, rhs, *exchange_fine(g, gx, *state))
    around = exchange_fine(g, gx, *state)
    (solution,) = call(kernel_scatter, [right_side.shape], [], state[0])
    (residual,) = call(kernel_last, [right_side.shape], [], g, rhs, *around)
    return solution, residual


def solution(mesh):
    return jax.shard_map(
        local,
        mesh=mesh,
        in_specs=(
            P(None, None, "ta", "gz", "xy", None),
            P(None, None, "ta", "gz", "xy", None),
            P(None, "ta", "gz", "xy", None),
            P(None, "ta", "gz", "xy", None),
            P(None, None, "ta", "gz", "xy", None),
            P(None, "ta", "gz", "xy", None),
            P(None, "ta", "gz", "xy", None),
            P(None, None, "ta", "gz", "xy", None, None),
            P(None, "ta", "gz", "xy", None, None),
        ),
        out_specs=(P(None, None, "ta", "gz", "xy", None), P(None, None, "ta", "gz", "xy", None)),
        check_vma=False,
    )
```

```python
import jax
import jax.numpy as jnp
from jax import lax
from jax.sharding import PartitionSpec as P
import jax.experimental.pallas as pl
from jax.experimental.pallas import tpu as pltpu

SWEEPS = 4
CYCLES = 2
F32 = jnp.float32
BF16 = jnp.bfloat16
HIGHEST = lax.Precision.HIGHEST
LANE_BITS = (64, 32, 16)
ROW_BITS = (4, 2, 1)
VMEM_BYTES = 24 << 20


class Site:
    def __init__(self):
        self.lane = lax.broadcasted_iota(jnp.int32, (8, 128), 1)
        self.row = lax.broadcasted_iota(jnp.int32, (8, 128), 0)
        self.by = self.lane & 7

    def lane_bit(self, d):
        return (self.lane & d) != 0

    def row_bit(self, d):
        return (self.row & d) != 0

    def first(self, direction):
        return ((self.lane & LANE_BITS[direction]) | (self.row & ROW_BITS[direction])) == 0

    def last(self, direction):
        return self.lane_bit(LANE_BITS[direction]) & self.row_bit(ROW_BITS[direction])


def left(x, s):
    s = s % 128
    return pltpu.roll(x, (128 - s) % 128, 1) if s else x


def up(x, s):
    s = s % 8
    return pltpu.roll(x, (8 - s) % 8, 0) if s else x


def flip_lane(site, x, d):
    if d == 64:
        return left(x, 64)
    return jnp.where(site.lane_bit(d), left(x, -d), left(x, d))


def flip_row(site, x, d):
    if d == 4:
        return up(x, 4)
    return jnp.where(site.row_bit(d), up(x, -d), up(x, d))


def cyclic(site, x, direction, sign):
    d = LANE_BITS[direction]
    flipped = flip_lane(site, x, d)
    both = flip_row(site, flipped, ROW_BITS[direction])
    if sign > 0:
        return jnp.where(site.lane_bit(d), both, flipped)
    return jnp.where(site.lane_bit(d), flipped, both)


def by_roll(site, x, base, q):
    moved = left(x, base + q)
    if q == 0:
        return moved
    if q > 0:
        return jnp.where(site.by >= 8 - q, left(x, base + q - 8), moved)
    return jnp.where(site.by < -q, left(x, base + q + 8), moved)


def shift_y(site, x, n):
    found = []
    for c in (0, 1):
        c_new = (c + n) % 2
        q = (c + n - c_new) // 2
        found.append(by_roll(site, x, 8 * (c_new - c), q))
    return jnp.where(site.lane_bit(8), found[1], found[0])


def link(links_ref, mu, kind, part, r, c):
    return links_ref[((mu * 2 + kind) * 2 + part) * 9 + r * 3 + c]


def link_apply(links_ref, mu, kind, field):
    out = [None] * 6
    for r in range(3):
        re = im = None
        for c in range(3):
            g_re = link(links_ref, mu, kind, 0, r, c)
            g_im = link(links_ref, mu, kind, 1, r, c)
            a = g_re * field[c] - g_im * field[3 + c]
            b = g_re * field[3 + c] + g_im * field[c]
            re = a if re is None else re + a
            im = b if im is None else im + b
        out[r] = re
        out[3 + r] = im
    return out


def link_adjoint(links_ref, mu, kind, field):
    out = [None] * 6
    for c in range(3):
        re = im = None
        for r in range(3):
            g_re = link(links_ref, mu, kind, 0, r, c)
            g_im = link(links_ref, mu, kind, 1, r, c)
            a = g_re * field[r] + g_im * field[3 + r]
            b = g_re * field[3 + r] - g_im * field[r]
            re = a if re is None else re + a
            im = b if im is None else im + b
        out[c] = re
        out[3 + c] = im
    return out


def add(xs, ys):
    return [x + y for x, y in zip(xs, ys)]


def sub(xs, ys):
    return [x - y for x, y in zip(xs, ys)]


def fine_send(site, links_ref, field):
    sent = []
    for direction in range(2):
        near, far = backward(site, links_ref, field, direction)
        first = site.first(direction)
        sent.append([jnp.where(first, n, f) for n, f in zip(near, far)])
    return sent


def fine_own(site, links_ref, field):
    acc = list(field)
    for kind, reach in ((0, 1), (1, 3)):
        acc = add(acc, link_apply(links_ref, 3, kind, [shift_y(site, x, reach) for x in field]))
        back = link_adjoint(links_ref, 3, kind, field)
        acc = sub(acc, [shift_y(site, x, -reach) for x in back])
    for direction in range(3):
        near, far = backward(site, links_ref, field, direction)
        first, last = site.first(direction), site.last(direction)
        acc = [
            a - jnp.where(first, 0.0, n) - jnp.where(last, cyclic(site, f, direction, 1), 0.0)
            for a, n, f in zip(acc, near, far)
        ]
    return acc


class PairedLinks:
    def __init__(self, ref):
        self.ref = ref

    def __getitem__(self, i):
        i -= 72
        return self.ref[i // 2].astype(F32)[8 * (i % 2) : 8 * (i % 2) + 8]


def backward(site, links_ref, field, direction):
    near = [cyclic(site, x, direction, -1) for x in link_adjoint(links_ref, direction, 0, field)]
    return near, link_adjoint(links_ref, direction, 1, field)


def fine_receive(site, links_ref, field, acc, ahead, behind):
    out = acc
    for direction in range(3):
        first, last = site.first(direction), site.last(direction)
        nxt = ahead[direction]
        one = [cyclic(site, jnp.where(first, n, x), direction, 1) for n, x in zip(nxt, field)]
        out = add(out, link_apply(links_ref, direction, 0, one))
        three = [cyclic(site, jnp.where(last, x, n), direction, -1) for n, x in zip(nxt, field)]
        out = add(out, link_apply(links_ref, direction, 1, three))
        out = [
            o - jnp.where(first, b, 0.0) - jnp.where(last, 0.0, cyclic(site, b, direction, 1))
            for o, b in zip(out, behind[direction])
        ]
    return out


def merge(site, d, a, b):
    bit = site.lane_bit(d)
    return jnp.where(bit, b, a) + left(jnp.where(bit, a, b), d)


def tree(site, leaf, base, n):
    if n == 2:
        a, b = leaf(base)
    else:
        a = tree(site, leaf, base, n // 2)
        b = tree(site, leaf, base + n // 2, n // 2)
    return [merge(site, 4 * n, x, y) for x, y in zip(a, b)]


def two_rows(ref, o):
    return ref[pl.ds(o * 8, 16), :].astype(F32)


def dot_tiles(block, row, x):
    total = None
    for j, v in enumerate(x):
        term = block[row : row + 8, 128 * j : 128 * j + 128] * v
        total = term if total is None else total + term
    return total


def pair_leaf(terms):
    def leaf(o):
        sums = [[None, None], [None, None]]
        for ref, base, x_re, x_im in terms:
            block = two_rows(ref, base + o)
            for h in range(2):
                for p, x in enumerate((x_re, x_im)):
                    t = dot_tiles(block, 8 * h, x)
                    sums[h][p] = t if sums[h][p] is None else sums[h][p] + t
        return sums

    return leaf


def fine_matrix(site, ref, field):
    x_re = field[:3] + [-x for x in field[3:]]
    x_im = field[3:] + field[:3]
    out = [tree(site, pair_leaf([(ref, 0, x_re, x_im)]), 16 * c, 16) for c in range(3)]
    return [o[0] for o in out] + [o[1] for o in out]


def mid_gather(site, terms):
    leaf = pair_leaf(terms)
    eight = [tree(site, leaf, 8 * j, 8) for j in range(3)]
    return [
        merge(site, 64, eight[0][0], eight[1][0]),
        merge(site, 64, eight[2][0], eight[0][1]),
        merge(site, 64, eight[1][1], eight[2][1]),
    ]


def swap_parts(site, v):
    low = jnp.logical_not(site.lane_bit(64))
    r = [left(x, 64) for x in v]
    return [jnp.where(low, r[1], r[2]), jnp.where(low, r[2], r[0]), jnp.where(low, r[0], r[1])]


def im_negated(site, v):
    return [v[0], jnp.where(site.lane_bit(64), -v[1], v[1]), -v[2]]


def mid_x(site, v):
    return im_negated(site, v), swap_parts(site, v)


def mid_x_conj(site, v):
    return v, im_negated(site, swap_parts(site, v))


def restrict_fine(site, near_ref, field):
    x_im = field[3:] + [-x for x in field[:3]]
    return mid_gather(site, [(near_ref, 0, field, x_im)])


def mid_matrix(site, ref, v):
    x_re, x_im = mid_x(site, v)
    return mid_gather(site, [(ref, 0, x_re, x_im)])


def mid_stencil_own(site, ref, v):
    shifted = ((0, v), (7, [by_roll(site, x, 0, 1) for x in v]), (8, [by_roll(site, x, 0, -1) for x in v]))
    return mid_gather(site, [(ref, 24 * k) + mid_x(site, s) for k, s in shifted])


def mid_stencil_near(site, ref, v, ahead, behind):
    shifted = []
    for direction in range(3):
        d = ROW_BITS[direction]
        bit = site.row_bit(d)
        shifted.append([flip_row(site, jnp.where(bit, x, n), d) for x, n in zip(v, ahead[direction])])
        shifted.append([flip_row(site, jnp.where(bit, n, x), d) for x, n in zip(v, behind[direction])])
    return mid_gather(site, [(ref, 24 * k + 24) + mid_x(site, s) for k, s in enumerate(shifted)])


def spread(site, v, ref):
    def down(x, base, d):
        if d == 4:
            ref[base] = x
            return
        bit = site.lane_bit(d)
        r = left(x, d)
        down(jnp.where(bit, r, x), base, d // 2)
        down(jnp.where(bit, x, r), base + d // 8, d // 2)

    for j, x in enumerate(v):
        down(x, 16 * j, 64)


def prolong_fine(site, near_ref, v, spread_ref):
    spread(site, v, spread_ref)
    a, b = [0.0] * 6, [0.0] * 6
    for o in range(0, 24, 2):
        block = two_rows(near_ref, o)
        for h in range(2):
            y_re, y_im = spread_ref[o + h], spread_ref[24 + o + h]
            for j in range(6):
                n = block[8 * h : 8 * h + 8, 128 * j : 128 * j + 128]
                a[j] = a[j] + n * y_re
                b[j] = b[j] + n * y_im
    return [a[j] - b[3 + j] for j in range(3)] + [a[3 + j] + b[j] for j in range(3)]


def iota2(shape, axis):
    return lax.broadcasted_iota(jnp.int32, shape, axis)


def pick_y(part):
    row, lane = iota2((8, 128), 0), iota2((8, 128), 1)
    return (row == part * 4 + (lane & 3)).astype(F32)


def permute_eight(site, x, source):
    out = x
    for move in sorted({s - i for i, s in enumerate(source)} - {0}):
        hit = None
        for i, s in enumerate(source):
            if s - i == move:
                hit = (site.by == i) if hit is None else hit | (site.by == i)
        out = jnp.where(hit, left(x, move), out)
    return out


SPLIT_Y = (0, 2, 4, 6, 1, 3, 5, 7)
JOIN_Y = (0, 4, 1, 5, 2, 6, 3, 7)


def total_rows(x):
    for d in (4, 2, 1):
        x = x + up(x, d)
    return x


def widen(site, v):
    own = ((site.lane >> 3) & 7) == site.row
    half = site.lane_bit(64) == site.lane_bit(8)
    found = []

    def down(x, d):
        if d == 8:
            x = jnp.where(half, x, flip_lane(site, x, 8))
            found.append(total_rows(jnp.where(own, x, 0.0)))
            return
        bit = site.lane_bit(d)
        r = left(x, d)
        down(jnp.where(bit, r, x), d // 2)
        down(jnp.where(bit, x, r), d // 2)

    for x in v:
        down(permute_eight(site, x, SPLIT_Y), 64)
    return found


def narrow(site, tiles):
    own = ((site.lane >> 3) & 7) == site.row
    same = site.lane_bit(64) == site.lane_bit(8)

    def fold(d, a, b):
        bit = site.lane_bit(d)
        return jnp.where(bit, b, a) + flip_lane(site, jnp.where(bit, a, b), d)

    out = []
    for q in range(0, 24, 8):
        t = [jnp.where(own, total_rows(x), 0.0) for x in tiles[q : q + 8]]
        t = [fold(8, t[i], t[i + 4]) for i in range(4)]
        t = [fold(32, t[i], t[i + 2]) for i in range(2)]
        x = fold(16, t[0], t[1])
        x = jnp.where(same, x, jnp.where(site.lane_bit(64), left(x, -56), left(x, 56)))
        out.append(permute_eight(site, x, JOIN_Y))
    return out


def restrict_mid(site, near_ref, v, tile_ref):
    x = widen(site, v)
    x_im = x[12:] + [-t for t in x[:12]]
    for o in range(0, 48, 16):
        re = [None, None]
        im = [None, None]
        for j in range(24):
            n = near_ref[pl.ds(o, 16), pl.ds(128 * j, 128)].astype(F32)
            for h in range(2):
                block = n[8 * h : 8 * h + 8]
                a, b = block * x[j], block * x_im[j]
                re[h] = a if re[h] is None else re[h] + a
                im[h] = b if im[h] is None else im[h] + b
        for h in range(2):
            tile_ref[0, pl.ds(o + 8 * h, 8), :] = re[h]
            tile_ref[1, pl.ds(o + 8 * h, 8), :] = im[h]
    dims = (((1,), (1,)), ((), ()))
    z = None
    for p in range(2):
        t = lax.dot_general(pick_y(p), tile_ref[p], dims, precision=HIGHEST, preferred_element_type=F32)
        z = t if z is None else z + t
    return z


def prolong_mid(site, near_ref, y3, row_ref):
    dims = (((0,), (0,)), ((), ()))
    for p in range(2):
        row_ref[p] = lax.dot_general(y3, pick_y(p), dims, precision=HIGHEST, preferred_element_type=F32)
    a, b = [None] * 24, [None] * 24
    for j in range(24):
        for o in range(0, 48, 16):
            n = near_ref[pl.ds(o, 16), pl.ds(128 * j, 128)].astype(F32)
            for h in range(2):
                block = n[8 * h : 8 * h + 8]
                s = block * row_ref[0, pl.ds(o + 8 * h, 8), :]
                t = block * row_ref[1, pl.ds(o + 8 * h, 8), :]
                a[j] = s if a[j] is None else a[j] + s
                b[j] = t if b[j] is None else b[j] + t
    tiles = [a[j] - b[12 + j] for j in range(12)] + [a[12 + j] + b[j] for j in range(12)]
    return narrow(site, tiles)


def coarse_rows(v):
    high = v.astype(BF16).astype(F32)
    return jnp.concatenate([high, v - high], axis=0).astype(BF16)


def coarse_matrix(terms):
    row = iota2((8, 48), 0)
    total = None
    for ref, base, v in terms:
        turned = jnp.where(row < 4, -up(v, 4), up(v, 4))
        for a, x in enumerate((v, turned)):
            t = jnp.dot(coarse_rows(x), ref[pl.ds(base + 48 * a, 48), :], preferred_element_type=F32)
            total = t if total is None else total + t
    both = total[:8] + total[8:]
    out = None
    for y in range(4):
        t = jnp.where((row & 3) == y, both[:, 48 * y : 48 * y + 48], 0.0)
        out = t if out is None else out + t
    return out


def coarse_stencil_own(ref, v):
    y = iota2((8, 48), 0) & 3
    up_y = jnp.where(y == 3, up(v, -3), up(v, 1))
    down_y = jnp.where(y == 0, up(v, 3), up(v, -1))
    return coarse_matrix([(ref, 0, v), (ref, 96 * 7, up_y), (ref, 96 * 8, down_y)])


def coarse_stencil_near(ref, ahead, behind):
    terms = []
    for direction in range(3):
        terms.append((ref, 96 * (2 * direction + 1), ahead[direction]))
        terms.append((ref, 96 * (2 * direction + 2), behind[direction]))
    return coarse_matrix(terms)


def load(ref, n, base=0):
    return [ref[base + i] for i in range(n)]


def store(ref, values, base=0):
    for i, x in enumerate(values):
        ref[base + i] = x


def is_odd(axis):
    return lax.rem(lax.axis_index(axis), 2) == 1


def finish_fine(site, links_ref, solution, sol_ref, z0_ref, z1_ref, t0_ref, t1_ref):
    store(sol_ref, solution)
    back_t, back_z = fine_send(site, links_ref, solution)
    for axis, back, ref0, ref1 in (("gz", back_z, z0_ref, z1_ref), ("ta", back_t, t0_ref, t1_ref)):
        odd = is_odd(axis)
        store(ref0, [jnp.where(odd, s, b) for s, b in zip(solution, back)])
        store(ref1, [jnp.where(odd, b, s) for s, b in zip(solution, back)])


def by_parity(axis, zero, one):
    odd = is_odd(axis)
    ahead = [jnp.where(odd, b, a) for a, b in zip(zero, one)]
    return ahead, [jnp.where(odd, a, b) for a, b in zip(zero, one)]


def begin_fine(site, links_ref, refs):
    sol_ref, acc_ref, t0, z1, z0, t1, x, gx_ref = refs
    solution = load(sol_ref, 6)
    ahead_t, behind_t = by_parity("ta", load(t0, 6), load(t1, 6))
    ahead_z, behind_z = by_parity("gz", load(z0, 6), load(z1, 6))
    ahead = [ahead_t, ahead_z, load(x, 6)]
    near, far = backward(site, PairedLinks(gx_ref), ahead[2], 2)
    first = site.first(2)
    behind = [behind_t, behind_z, [jnp.where(first, n, f) for n, f in zip(near, far)]]
    return solution, fine_receive(site, links_ref, solution, load(acc_ref, 6), ahead, behind)


def row_order(transposed):
    m, n = iota2((64, 64), 0), iota2((64, 64), 1)
    if transposed:
        m, n = n, m
    bit = lambda v, k: (v >> k) & 1
    fine = (
        (bit(m, 2) << 5) | (bit(m, 5) << 4) | (bit(m, 1) << 3) | (bit(m, 4) << 2) | (bit(m, 0) << 1) | bit(m, 3)
    )
    return n == fine


def y_order(rows, columns, transposed):
    m, n = iota2((rows, columns), 0), iota2((rows, columns), 1)
    if transposed:
        m, n = n, m
    fine = (((n & 7) << 1) | ((n >> 3) & 1)) | (n & 112)
    return (m == (fine & (min(rows, columns) - 1))).astype(BF16)


def dot(a, b):
    return jnp.dot(a, b, preferred_element_type=F32)


def three_parts(x):
    high = x.astype(BF16)
    rest = x - high.astype(F32)
    mid = rest.astype(BF16)
    return high, mid, (rest - mid.astype(F32)).astype(BF16)


def prepare_links(site, links_ref, g_ref, gx_ref):
    rows = row_order(False).astype(BF16)
    lanes = y_order(128, 128, False)
    signs = [jnp.full((8, 128), 0.5, F32)]
    for d in LANE_BITS:
        signs.append(jnp.where(site.lane_bit(d), -signs[-1], signs[-1]))
    for rc in range(9):
        parts = [links_ref[rc // 3, rc % 3, t, z].astype(F32) for t in range(4) for z in range(4)]
        block = dot(rows, jnp.concatenate(parts, axis=0).astype(BF16)).astype(BF16)
        for h in range(2):
            half = dot(block[:, 128 * h : 128 * h + 128], lanes)
            v = [half[8 * w : 8 * w + 8] for w in range(8)]
            for d, k in zip(LANE_BITS, (4, 2, 1)):
                bit = site.lane_bit(d)
                for w in range(8):
                    if not w & k:
                        lo, hi = v[w], v[w | k]
                        v[w] = jnp.where(bit, left(hi, -d), lo)
                        v[w | k] = jnp.where(bit, hi, left(lo, d))
            for m in range(8):
                g_ref[(8 * h + m) * 9 + rc] = v[m] * signs[2 * h + m // 4]
    for i in range(0, 36, 2):
        gx_ref[i // 2] = jnp.concatenate([g_ref[72 + i], g_ref[73 + i]], axis=0).astype(BF16)


def gather_fine(site, field_ref):
    rows = row_order(False).astype(BF16)
    lanes = y_order(16, 128, False)
    group = site.lane >> 4
    out = []
    for p in range(2):
        for c in range(3):
            parts = [field_ref[p, c, t, z] for t in range(4) for z in range(4)]
            moved = [dot(rows, x) for x in three_parts(jnp.concatenate(parts, axis=0))]
            wide = dot(jnp.concatenate(moved, axis=0).astype(BF16), lanes)
            total = None
            for w in range(8):
                own = wide[8 * w : 8 * w + 8] + wide[64 + 8 * w : 72 + 8 * w] + wide[128 + 8 * w : 136 + 8 * w]
                total = own if w == 0 else jnp.where(group == w, own, total)
            out.append(total)
    return out


def scatter_fine(site, field, out_ref):
    rows = row_order(True).astype(F32)
    rows = jnp.concatenate([rows, rows, rows], axis=1).astype(BF16)
    lanes = y_order(128, 16, True)
    group = site.lane >> 4
    for p in range(2):
        for c in range(3):
            parts = [x.astype(F32) for x in three_parts(field[3 * p + c])]
            tall = jnp.concatenate([jnp.where(group == w, x, 0.0) for x in parts for w in range(8)], axis=0)
            value = dot(rows, dot(tall.astype(BF16), lanes).astype(BF16))
            for t in range(4):
                for z in range(4):
                    out_ref[p, c, t, z] = value[16 * t + 4 * z : 16 * t + 4 * z + 4]


def kernel_links(links_ref, g_ref, gx_ref):
    prepare_links(Site(), links_ref, g_ref, gx_ref)


def kernel_first(g_ref, block_ref, source_ref, rhs_ref, *outs):
    site = Site()
    rhs = gather_fine(site, source_ref)
    store(rhs_ref, rhs)
    finish_fine(site, g_ref, fine_matrix(site, block_ref, rhs), *outs)


def kernel_smooth(links_ref, block_ref, rhs_ref, *refs):
    site = Site()
    solution, applied = begin_fine(site, links_ref, refs[:8])
    residual = sub(load(rhs_ref, 6), applied)
    solution = add(solution, fine_matrix(site, block_ref, residual))
    finish_fine(site, links_ref, solution, *refs[8:])


def kernel_last(links_ref, rhs_ref, *refs):
    site = Site()
    _, applied = begin_fine(site, links_ref, refs[:8])
    scatter_fine(site, sub(load(rhs_ref, 6), applied), refs[8])


def kernel_own(links_ref, field_ref, acc_ref):
    store(acc_ref, fine_own(Site(), links_ref, load(field_ref, 6)))


def kernel_scatter(field_ref, out_ref):
    scatter_fine(Site(), load(field_ref, 6), out_ref)


def kernel_restrict(links_ref, near_ref, jacobi_ref, rhs_ref, *refs):
    site = Site()
    _, applied = begin_fine(site, links_ref, refs[:8])
    residual = sub(load(rhs_ref, 6), applied)
    mid_res = restrict_fine(site, near_ref, residual)
    store(refs[8], mid_res)
    store(refs[9], mid_matrix(site, jacobi_ref, mid_res))


def neighbours(refs, get):
    nx, t1, z0, z1, t0 = refs
    ahead_t, behind_t = by_parity("ta", get(t0), get(t1))
    ahead_z, behind_z = by_parity("gz", get(z0), get(z1))
    return [ahead_t, ahead_z, get(nx)], [behind_t, behind_z, get(nx)]


def kernel_mid_own(stencil_ref, v_ref, out_ref):
    site = Site()
    store(out_ref, mid_stencil_own(site, stencil_ref, load(v_ref, 3)))


def mid_rest(site, stencil_ref, res_ref, y2_ref, own_ref, around):
    ahead, behind = neighbours(around, lambda r: load(r, 3))
    applied = mid_stencil_near(site, stencil_ref, load(y2_ref, 3), ahead, behind)
    return sub(load(res_ref, 3), add(load(own_ref, 3), applied))


def kernel_mid_down(stencil_ref, near_ref, jacobi_ref, res_ref, y2_ref, own_ref, *refs):
    site = Site()
    around, (r3_ref, y3_ref, tile_ref) = refs[:-3], refs[-3:]
    rest = mid_rest(site, stencil_ref, res_ref, y2_ref, own_ref, around)
    r3 = restrict_mid(site, near_ref, rest, tile_ref)
    r3_ref[...] = r3
    y3_ref[...] = coarse_matrix([(jacobi_ref, 0, r3)])


def kernel_sweep_own(stencil_ref, r3_ref, y3_ref, out_ref):
    out_ref[...] = r3_ref[...] - coarse_stencil_own(stencil_ref, y3_ref[...])


def sweep(stencil_ref, jacobi_ref, own_ref, y3_ref, around):
    ahead, behind = neighbours(around, lambda r: [r[...]])
    ahead, behind = [x[0] for x in ahead], [x[0] for x in behind]
    rest = own_ref[...] - coarse_stencil_near(stencil_ref, ahead, behind)
    return y3_ref[...] + coarse_matrix([(jacobi_ref, 0, rest)])


def kernel_sweep(stencil_ref, jacobi_ref, own_ref, y3_ref, *refs):
    refs[-1][...] = sweep(stencil_ref, jacobi_ref, own_ref, y3_ref, refs[:-1])


def kernel_sweep_up(stencil_ref, jacobi_ref, near_ref, y2_ref, own_ref, y3_ref, *refs):
    site = Site()
    around, (out_ref, row_ref) = refs[:-2], refs[-2:]
    y3 = sweep(stencil_ref, jacobi_ref, own_ref, y3_ref, around)
    store(out_ref, add(load(y2_ref, 3), prolong_mid(site, near_ref, y3, row_ref)))


def kernel_mid_up(links_ref, stencil_ref, jacobi_ref, near_ref, old_ref, res_ref, y2_ref, own_ref, *refs):
    site = Site()
    around, outs, spread_ref = refs[:-6], refs[-6:-1], refs[-1]
    rest = mid_rest(site, stencil_ref, res_ref, y2_ref, own_ref, around)
    y2 = add(load(y2_ref, 3), mid_matrix(site, jacobi_ref, rest))
    solution = add(load(old_ref, 6), prolong_fine(site, near_ref, y2, spread_ref))
    finish_fine(site, links_ref, solution, *outs)


def call(kernel, outs, scratch, *args, after=()):
    def body(*refs):
        kernel(*refs[len(after) :])

    specs = [pl.BlockSpec(memory_space=pl.ANY)] * len(after)
    return pl.pallas_call(
        body,
        out_shape=[jax.ShapeDtypeStruct(*s) if s[1] == BF16 else jax.ShapeDtypeStruct(s, F32) for s in outs],
        in_specs=specs + [pl.BlockSpec(memory_space=pltpu.VMEM)] * len(args),
        scratch_shapes=[pltpu.VMEM(s, F32) for s in scratch],
        compiler_params=pltpu.CompilerParams(vmem_limit_bytes=VMEM_BYTES),
        name=kernel.__name__,
    )(*after, *args)


def from_behind(block, axis, distance):
    n = lax.axis_size(axis)
    return lax.ppermute(block, axis, [((i - distance) % n, i) for i in range(n)])


def swap(block, axis, phase):
    n = lax.axis_size(axis)
    return lax.ppermute(block, axis, [(i, (((i + phase) ^ 1) - phase) % n) for i in range(n)])


def exchange(v):
    x = from_behind(v, "xy", 1)
    t1 = swap(v, "ta", 1)
    z0 = swap(v, "gz", 0)
    z1 = swap(v, "gz", 1)
    t0 = swap(v, "ta", 0)
    return [x, t1, z0, z1, t0]


def exchange_fine(g, gx, sol, z0, z1, t0, t1):
    x = from_behind(sol, "xy", 1)
    t1 = swap(t1, "ta", 1)
    z0 = swap(z0, "gz", 0)
    z1 = swap(z1, "gz", 1)
    t0 = swap(t0, "ta", 0)
    (acc,) = call(kernel_own, [TILE6], [], g, sol)
    return [sol, acc, t0, z1, z0, t1, x, gx]


TILE6 = (6, 8, 128)
FINE_OUT = [TILE6] * 5


def local(
    right_side,
    links,
    block_inverse,
    near_fine,
    mid_stencil,
    mid_jacobi,
    near_mid,
    coarse_stencil,
    coarse_jacobi,
):
    block = block_inverse.reshape(384, 768)
    near1 = near_fine.reshape(192, 768)
    stencil2 = mid_stencil.reshape(1728, 384)
    jacobi2 = mid_jacobi.reshape(192, 384)
    near2 = near_mid.reshape(near_mid.shape[0], near_mid.shape[4])
    stencil3 = jnp.swapaxes(coarse_stencil, 5, 6).reshape(864, 192)
    jacobi3 = jnp.swapaxes(coarse_jacobi, 4, 5).reshape(96, 192)
    mid = (3, 8, 128)
    coarse = (8, 48)

    g, gx = call(kernel_links, [(144, 8, 128), ((18, 16, 128), BF16)], [], links, after=(block,))
    gx = from_behind(gx, "xy", 1)
    rhs, *state = call(kernel_first, [TILE6] + FINE_OUT, [], g, block, right_side)
    for cycle_no in range(CYCLES):
        around = exchange_fine(g, gx, *state)
        r2, y2 = call(kernel_restrict, [mid, mid], [], g, near1, jacobi2, rhs, *around, after=(stencil2,))
        around = exchange(y2)
        (own,) = call(kernel_mid_own, [mid], [], stencil2, y2)
        r3, y3 = call(
            kernel_mid_down, [coarse, coarse], [(2, 48, 128)], stencil2, near2, jacobi3, r2, y2, own, *around
        )
        for _ in range(SWEEPS - 1):
            around = exchange(y3)
            (own,) = call(kernel_sweep_own, [coarse], [], stencil3, r3, y3)
            (y3,) = call(kernel_sweep, [coarse], [], stencil3, jacobi3, own, y3, *around)
        around = exchange(y3)
        (own,) = call(kernel_sweep_own, [coarse], [], stencil3, r3, y3)
        (y2,) = call(
            kernel_sweep_up, [mid], [(2, 48, 128)], stencil3, jacobi3, near2, y2, own, y3, *around
        )
        around = exchange(y2)
        (own,) = call(kernel_mid_own, [mid], [], stencil2, y2)
        state = call(
            kernel_mid_up,
            FINE_OUT,
            [(48, 8, 128)],
            g,
            stencil2,
            jacobi2,
            near1,
            state[0],
            r2,
            y2,
            own,
            *around,
        )
        state = call(kernel_smooth, FINE_OUT, [], g, block, rhs, *exchange_fine(g, gx, *state))
        if cycle_no < CYCLES - 1:
            state = call(kernel_smooth, FINE_OUT, [], g, block, rhs, *exchange_fine(g, gx, *state))
    around = exchange_fine(g, gx, *state)
    (solution,) = call(kernel_scatter, [right_side.shape], [], state[0])
    (residual,) = call(kernel_last, [right_side.shape], [], g, rhs, *around)
    return solution, residual


def solution(mesh):
    return jax.shard_map(
        local,
        mesh=mesh,
        in_specs=(
            P(None, None, "ta", "gz", "xy", None),
            P(None, None, "ta", "gz", "xy", None),
            P(None, "ta", "gz", "xy", None),
            P(None, "ta", "gz", "xy", None),
            P(None, None, "ta", "gz", "xy", None),
            P(None, "ta", "gz", "xy", None),
            P(None, "ta", "gz", "xy", None),
            P(None, None, "ta", "gz", "xy", None, None),
            P(None, "ta", "gz", "xy", None, None),
        ),
        out_specs=(P(None, None, "ta", "gz", "xy", None), P(None, None, "ta", "gz", "xy", None)),
        check_vma=False,
    )
```

```python
import jax
import jax.numpy as jnp
from jax import lax
from jax.sharding import PartitionSpec as P
import jax.experimental.pallas as pl
from jax.experimental.pallas import tpu as pltpu

SWEEPS = 4
CYCLES = 2
F32 = jnp.float32
BF16 = jnp.bfloat16
HIGHEST = lax.Precision.HIGHEST
LANE_BITS = (64, 32, 16)
ROW_BITS = (4, 2, 1)
VMEM_BYTES = 24 << 20


class Site:
    def __init__(self):
        self.lane = lax.broadcasted_iota(jnp.int32, (8, 128), 1)
        self.row = lax.broadcasted_iota(jnp.int32, (8, 128), 0)
        self.by = self.lane & 7

    def lane_bit(self, d):
        return (self.lane & d) != 0

    def row_bit(self, d):
        return (self.row & d) != 0

    def first(self, direction):
        return ((self.lane & LANE_BITS[direction]) | (self.row & ROW_BITS[direction])) == 0

    def last(self, direction):
        return self.lane_bit(LANE_BITS[direction]) & self.row_bit(ROW_BITS[direction])


def left(x, s):
    s = s % 128
    return pltpu.roll(x, (128 - s) % 128, 1) if s else x


def up(x, s):
    s = s % 8
    return pltpu.roll(x, (8 - s) % 8, 0) if s else x


def flip_lane(site, x, d):
    if d == 64:
        return left(x, 64)
    return jnp.where(site.lane_bit(d), left(x, -d), left(x, d))


def flip_row(site, x, d):
    if d == 4:
        return up(x, 4)
    return jnp.where(site.row_bit(d), up(x, -d), up(x, d))


def cyclic(site, x, direction, sign):
    d = LANE_BITS[direction]
    flipped = flip_lane(site, x, d)
    both = flip_row(site, flipped, ROW_BITS[direction])
    if sign > 0:
        return jnp.where(site.lane_bit(d), both, flipped)
    return jnp.where(site.lane_bit(d), flipped, both)


def by_roll(site, x, base, q):
    moved = left(x, base + q)
    if q == 0:
        return moved
    if q > 0:
        return jnp.where(site.by >= 8 - q, left(x, base + q - 8), moved)
    return jnp.where(site.by < -q, left(x, base + q + 8), moved)


def shift_y(site, x, n):
    found = []
    for c in (0, 1):
        c_new = (c + n) % 2
        q = (c + n - c_new) // 2
        found.append(by_roll(site, x, 8 * (c_new - c), q))
    return jnp.where(site.lane_bit(8), found[1], found[0])


def link(links_ref, mu, kind, part, r, c):
    return links_ref[((mu * 2 + kind) * 2 + part) * 9 + r * 3 + c]


def link_apply(links_ref, mu, kind, field):
    out = [None] * 6
    for r in range(3):
        re = im = None
        for c in range(3):
            g_re = link(links_ref, mu, kind, 0, r, c)
            g_im = link(links_ref, mu, kind, 1, r, c)
            a = g_re * field[c] - g_im * field[3 + c]
            b = g_re * field[3 + c] + g_im * field[c]
            re = a if re is None else re + a
            im = b if im is None else im + b
        out[r] = re
        out[3 + r] = im
    return out


def link_adjoint(links_ref, mu, kind, field):
    out = [None] * 6
    for c in range(3):
        re = im = None
        for r in range(3):
            g_re = link(links_ref, mu, kind, 0, r, c)
            g_im = link(links_ref, mu, kind, 1, r, c)
            a = g_re * field[r] + g_im * field[3 + r]
            b = g_re * field[3 + r] - g_im * field[r]
            re = a if re is None else re + a
            im = b if im is None else im + b
        out[c] = re
        out[3 + c] = im
    return out


def add(xs, ys):
    return [x + y for x, y in zip(xs, ys)]


def sub(xs, ys):
    return [x - y for x, y in zip(xs, ys)]


def fine_send(site, links_ref, field):
    sent = []
    for direction in range(2):
        near, far = backward(site, links_ref, field, direction)
        first = site.first(direction)
        sent.append([jnp.where(first, n, f) for n, f in zip(near, far)])
    return sent


def fine_own(site, links_ref, field):
    acc = list(field)
    for kind, reach in ((0, 1), (1, 3)):
        acc = add(acc, link_apply(links_ref, 3, kind, [shift_y(site, x, reach) for x in field]))
        back = link_adjoint(links_ref, 3, kind, field)
        acc = sub(acc, [shift_y(site, x, -reach) for x in back])
    for direction in range(3):
        near, far = backward(site, links_ref, field, direction)
        first, last = site.first(direction), site.last(direction)
        acc = [
            a - jnp.where(first, 0.0, n) - jnp.where(last, cyclic(site, f, direction, 1), 0.0)
            for a, n, f in zip(acc, near, far)
        ]
    return acc


class PairedLinks:
    def __init__(self, ref):
        self.ref = ref

    def __getitem__(self, i):
        i -= 72
        return self.ref[i // 2].astype(F32)[8 * (i % 2) : 8 * (i % 2) + 8]


def backward(site, links_ref, field, direction):
    near = [cyclic(site, x, direction, -1) for x in link_adjoint(links_ref, direction, 0, field)]
    return near, link_adjoint(links_ref, direction, 1, field)


def fine_receive(site, links_ref, field, acc, ahead, behind):
    out = acc
    for direction in range(3):
        first, last = site.first(direction), site.last(direction)
        nxt = ahead[direction]
        one = [cyclic(site, jnp.where(first, n, x), direction, 1) for n, x in zip(nxt, field)]
        out = add(out, link_apply(links_ref, direction, 0, one))
        three = [cyclic(site, jnp.where(last, x, n), direction, -1) for n, x in zip(nxt, field)]
        out = add(out, link_apply(links_ref, direction, 1, three))
        out = [
            o - jnp.where(first, b, 0.0) - jnp.where(last, 0.0, cyclic(site, b, direction, 1))
            for o, b in zip(out, behind[direction])
        ]
    return out


def merge(site, d, a, b):
    bit = site.lane_bit(d)
    return jnp.where(bit, b, a) + left(jnp.where(bit, a, b), d)


def tree(site, leaf, base, n):
    if n == 2:
        a, b = leaf(base)
    else:
        a = tree(site, leaf, base, n // 2)
        b = tree(site, leaf, base + n // 2, n // 2)
    return [merge(site, 4 * n, x, y) for x, y in zip(a, b)]


def two_rows(ref, o):
    return ref[pl.ds(o * 8, 16), :].astype(F32)


def dot_tiles(block, row, x):
    total = None
    for j, v in enumerate(x):
        term = block[row : row + 8, 128 * j : 128 * j + 128] * v
        total = term if total is None else total + term
    return total


def pair_leaf(terms):
    def leaf(o):
        sums = [[None, None], [None, None]]
        for ref, base, x_re, x_im in terms:
            block = two_rows(ref, base + o)
            for h in range(2):
                for p, x in enumerate((x_re, x_im)):
                    t = dot_tiles(block, 8 * h, x)
                    sums[h][p] = t if sums[h][p] is None else sums[h][p] + t
        return sums

    return leaf


def fine_matrix(site, ref, field):
    x_re = field[:3] + [-x for x in field[3:]]
    x_im = field[3:] + field[:3]
    out = [tree(site, pair_leaf([(ref, 0, x_re, x_im)]), 16 * c, 16) for c in range(3)]
    return [o[0] for o in out] + [o[1] for o in out]


def mid_gather(site, terms):
    leaf = pair_leaf(terms)
    eight = [tree(site, leaf, 8 * j, 8) for j in range(3)]
    return [
        merge(site, 64, eight[0][0], eight[1][0]),
        merge(site, 64, eight[2][0], eight[0][1]),
        merge(site, 64, eight[1][1], eight[2][1]),
    ]


def swap_parts(site, v):
    low = jnp.logical_not(site.lane_bit(64))
    r = [left(x, 64) for x in v]
    return [jnp.where(low, r[1], r[2]), jnp.where(low, r[2], r[0]), jnp.where(low, r[0], r[1])]


def im_negated(site, v):
    return [v[0], jnp.where(site.lane_bit(64), -v[1], v[1]), -v[2]]


def mid_x(site, v):
    return im_negated(site, v), swap_parts(site, v)


def mid_x_conj(site, v):
    return v, im_negated(site, swap_parts(site, v))


def restrict_fine(site, near_ref, field):
    x_im = field[3:] + [-x for x in field[:3]]
    return mid_gather(site, [(near_ref, 0, field, x_im)])


def mid_matrix(site, ref, v):
    x_re, x_im = mid_x(site, v)
    return mid_gather(site, [(ref, 0, x_re, x_im)])


def mid_stencil_own(site, ref, v):
    shifted = ((0, v), (7, [by_roll(site, x, 0, 1) for x in v]), (8, [by_roll(site, x, 0, -1) for x in v]))
    return mid_gather(site, [(ref, 24 * k) + mid_x(site, s) for k, s in shifted])


def mid_stencil_near(site, ref, v, ahead, behind):
    shifted = []
    for direction in range(3):
        d = ROW_BITS[direction]
        bit = site.row_bit(d)
        shifted.append([flip_row(site, jnp.where(bit, x, n), d) for x, n in zip(v, ahead[direction])])
        shifted.append([flip_row(site, jnp.where(bit, n, x), d) for x, n in zip(v, behind[direction])])
    return mid_gather(site, [(ref, 24 * k + 24) + mid_x(site, s) for k, s in enumerate(shifted)])


def spread(site, v, ref):
    def down(x, base, d):
        if d == 4:
            ref[base] = x
            return
        bit = site.lane_bit(d)
        r = left(x, d)
        down(jnp.where(bit, r, x), base, d // 2)
        down(jnp.where(bit, x, r), base + d // 8, d // 2)

    for j, x in enumerate(v):
        down(x, 16 * j, 64)


def prolong_fine(site, near_ref, v, spread_ref):
    spread(site, v, spread_ref)
    a, b = [0.0] * 6, [0.0] * 6
    for o in range(0, 24, 2):
        block = two_rows(near_ref, o)
        for h in range(2):
            y_re, y_im = spread_ref[o + h], spread_ref[24 + o + h]
            for j in range(6):
                n = block[8 * h : 8 * h + 8, 128 * j : 128 * j + 128]
                a[j] = a[j] + n * y_re
                b[j] = b[j] + n * y_im
    return [a[j] - b[3 + j] for j in range(3)] + [a[3 + j] + b[j] for j in range(3)]


def iota2(shape, axis):
    return lax.broadcasted_iota(jnp.int32, shape, axis)


def pick_y(part):
    row, lane = iota2((8, 128), 0), iota2((8, 128), 1)
    return (row == part * 4 + (lane & 3)).astype(F32)


def permute_eight(site, x, source):
    out = x
    for move in sorted({s - i for i, s in enumerate(source)} - {0}):
        hit = None
        for i, s in enumerate(source):
            if s - i == move:
                hit = (site.by == i) if hit is None else hit | (site.by == i)
        out = jnp.where(hit, left(x, move), out)
    return out


SPLIT_Y = (0, 2, 4, 6, 1, 3, 5, 7)
JOIN_Y = (0, 4, 1, 5, 2, 6, 3, 7)


def total_rows(x):
    for d in (4, 2, 1):
        x = x + up(x, d)
    return x


def widen(site, v):
    own = ((site.lane >> 3) & 7) == site.row
    half = site.lane_bit(64) == site.lane_bit(8)
    found = []

    def down(x, d):
        if d == 8:
            x = jnp.where(half, x, flip_lane(site, x, 8))
            found.append(total_rows(jnp.where(own, x, 0.0)))
            return
        bit = site.lane_bit(d)
        r = left(x, d)
        down(jnp.where(bit, r, x), d // 2)
        down(jnp.where(bit, x, r), d // 2)

    for x in v:
        down(permute_eight(site, x, SPLIT_Y), 64)
    return found


def narrow(site, tiles):
    own = ((site.lane >> 3) & 7) == site.row
    same = site.lane_bit(64) == site.lane_bit(8)

    def fold(d, a, b):
        bit = site.lane_bit(d)
        return jnp.where(bit, b, a) + flip_lane(site, jnp.where(bit, a, b), d)

    out = []
    for q in range(0, 24, 8):
        t = [jnp.where(own, total_rows(x), 0.0) for x in tiles[q : q + 8]]
        t = [fold(8, t[i], t[i + 4]) for i in range(4)]
        t = [fold(32, t[i], t[i + 2]) for i in range(2)]
        x = fold(16, t[0], t[1])
        x = jnp.where(same, x, jnp.where(site.lane_bit(64), left(x, -56), left(x, 56)))
        out.append(permute_eight(site, x, JOIN_Y))
    return out


def restrict_mid(site, near_ref, v, tile_ref):
    x = widen(site, v)
    x_im = x[12:] + [-t for t in x[:12]]
    for o in range(0, 48, 16):
        re = [None, None]
        im = [None, None]
        for j in range(24):
            n = near_ref[pl.ds(o, 16), pl.ds(128 * j, 128)].astype(F32)
            for h in range(2):
                block = n[8 * h : 8 * h + 8]
                a, b = block * x[j], block * x_im[j]
                re[h] = a if re[h] is None else re[h] + a
                im[h] = b if im[h] is None else im[h] + b
        for h in range(2):
            tile_ref[0, pl.ds(o + 8 * h, 8), :] = re[h]
            tile_ref[1, pl.ds(o + 8 * h, 8), :] = im[h]
    dims = (((1,), (1,)), ((), ()))
    z = None
    for p in range(2):
        t = lax.dot_general(pick_y(p), tile_ref[p], dims, precision=HIGHEST, preferred_element_type=F32)
        z = t if z is None else z + t
    return z


def prolong_mid(site, near_ref, y3, row_ref):
    dims = (((0,), (0,)), ((), ()))
    for p in range(2):
        row_ref[p] = lax.dot_general(y3, pick_y(p), dims, precision=HIGHEST, preferred_element_type=F32)
    a, b = [None] * 24, [None] * 24
    for j in range(24):
        for o in range(0, 48, 16):
            n = near_ref[pl.ds(o, 16), pl.ds(128 * j, 128)].astype(F32)
            for h in range(2):
                block = n[8 * h : 8 * h + 8]
                s = block * row_ref[0, pl.ds(o + 8 * h, 8), :]
                t = block * row_ref[1, pl.ds(o + 8 * h, 8), :]
                a[j] = s if a[j] is None else a[j] + s
                b[j] = t if b[j] is None else b[j] + t
    tiles = [a[j] - b[12 + j] for j in range(12)] + [a[12 + j] + b[j] for j in range(12)]
    return narrow(site, tiles)


def coarse_rows(v):
    high = v.astype(BF16).astype(F32)
    return jnp.concatenate([high, v - high], axis=0).astype(BF16)


def coarse_matrix(terms):
    row = iota2((8, 48), 0)
    total = None
    for ref, base, v in terms:
        turned = jnp.where(row < 4, -up(v, 4), up(v, 4))
        for a, x in enumerate((v, turned)):
            t = jnp.dot(coarse_rows(x), ref[pl.ds(base + 48 * a, 48), :], preferred_element_type=F32)
            total = t if total is None else total + t
    both = total[:8] + total[8:]
    out = None
    for y in range(4):
        t = jnp.where((row & 3) == y, both[:, 48 * y : 48 * y + 48], 0.0)
        out = t if out is None else out + t
    return out


def coarse_stencil_own(ref, v):
    y = iota2((8, 48), 0) & 3
    up_y = jnp.where(y == 3, up(v, -3), up(v, 1))
    down_y = jnp.where(y == 0, up(v, 3), up(v, -1))
    return coarse_matrix([(ref, 0, v), (ref, 96 * 7, up_y), (ref, 96 * 8, down_y)])


def coarse_stencil_near(ref, ahead, behind):
    terms = []
    for direction in range(3):
        terms.append((ref, 96 * (2 * direction + 1), ahead[direction]))
        terms.append((ref, 96 * (2 * direction + 2), behind[direction]))
    return coarse_matrix(terms)


def load(ref, n, base=0):
    return [ref[base + i] for i in range(n)]


def store(ref, values, base=0):
    for i, x in enumerate(values):
        ref[base + i] = x


def is_odd(axis):
    return lax.rem(lax.axis_index(axis), 2) == 1


def finish_fine(site, links_ref, solution, sol_ref, z0_ref, z1_ref, t0_ref, t1_ref):
    store(sol_ref, solution)
    back_t, back_z = fine_send(site, links_ref, solution)
    for axis, back, ref0, ref1 in (("gz", back_z, z0_ref, z1_ref), ("ta", back_t, t0_ref, t1_ref)):
        odd = is_odd(axis)
        store(ref0, [jnp.where(odd, s, b) for s, b in zip(solution, back)])
        store(ref1, [jnp.where(odd, b, s) for s, b in zip(solution, back)])


def by_parity(axis, zero, one):
    odd = is_odd(axis)
    ahead = [jnp.where(odd, b, a) for a, b in zip(zero, one)]
    return ahead, [jnp.where(odd, a, b) for a, b in zip(zero, one)]


def begin_fine(site, links_ref, refs):
    sol_ref, acc_ref, t0, x, z1, z0, t1, gx_ref = refs
    solution = load(sol_ref, 6)
    ahead_t, behind_t = by_parity("ta", load(t0, 6), load(t1, 6))
    ahead_z, behind_z = by_parity("gz", load(z0, 6), load(z1, 6))
    ahead = [ahead_t, ahead_z, load(x, 6)]
    near, far = backward(site, PairedLinks(gx_ref), ahead[2], 2)
    first = site.first(2)
    behind = [behind_t, behind_z, [jnp.where(first, n, f) for n, f in zip(near, far)]]
    return solution, fine_receive(site, links_ref, solution, load(acc_ref, 6), ahead, behind)


def row_order(transposed):
    m, n = iota2((64, 64), 0), iota2((64, 64), 1)
    if transposed:
        m, n = n, m
    bit = lambda v, k: (v >> k) & 1
    fine = (
        (bit(m, 2) << 5) | (bit(m, 5) << 4) | (bit(m, 1) << 3) | (bit(m, 4) << 2) | (bit(m, 0) << 1) | bit(m, 3)
    )
    return n == fine


def y_order(rows, columns, transposed):
    m, n = iota2((rows, columns), 0), iota2((rows, columns), 1)
    if transposed:
        m, n = n, m
    fine = (((n & 7) << 1) | ((n >> 3) & 1)) | (n & 112)
    return (m == (fine & (min(rows, columns) - 1))).astype(BF16)


def dot(a, b):
    return jnp.dot(a, b, preferred_element_type=F32)


def three_parts(x):
    high = x.astype(BF16)
    rest = x - high.astype(F32)
    mid = rest.astype(BF16)
    return high, mid, (rest - mid.astype(F32)).astype(BF16)


def prepare_links(site, links_ref, g_ref, gx_ref):
    rows = row_order(False).astype(BF16)
    lanes = y_order(128, 128, False)
    signs = [jnp.full((8, 128), 0.5, F32)]
    for d in LANE_BITS:
        signs.append(jnp.where(site.lane_bit(d), -signs[-1], signs[-1]))
    for rc in range(9):
        parts = [links_ref[rc // 3, rc % 3, t, z].astype(F32) for t in range(4) for z in range(4)]
        block = dot(rows, jnp.concatenate(parts, axis=0).astype(BF16)).astype(BF16)
        for h in range(2):
            half = dot(block[:, 128 * h : 128 * h + 128], lanes)
            v = [half[8 * w : 8 * w + 8] for w in range(8)]
            for d, k in zip(LANE_BITS, (4, 2, 1)):
                bit = site.lane_bit(d)
                for w in range(8):
                    if not w & k:
                        lo, hi = v[w], v[w | k]
                        v[w] = jnp.where(bit, left(hi, -d), lo)
                        v[w | k] = jnp.where(bit, hi, left(lo, d))
            for m in range(8):
                g_ref[(8 * h + m) * 9 + rc] = v[m] * signs[2 * h + m // 4]
    for i in range(0, 36, 2):
        gx_ref[i // 2] = jnp.concatenate([g_ref[72 + i], g_ref[73 + i]], axis=0).astype(BF16)


def gather_fine(site, field_ref):
    rows = row_order(False).astype(BF16)
    lanes = y_order(16, 128, False)
    group = site.lane >> 4
    out = []
    for p in range(2):
        for c in range(3):
            parts = [field_ref[p, c, t, z] for t in range(4) for z in range(4)]
            moved = [dot(rows, x) for x in three_parts(jnp.concatenate(parts, axis=0))]
            wide = dot(jnp.concatenate(moved, axis=0).astype(BF16), lanes)
            total = None
            for w in range(8):
                own = wide[8 * w : 8 * w + 8] + wide[64 + 8 * w : 72 + 8 * w] + wide[128 + 8 * w : 136 + 8 * w]
                total = own if w == 0 else jnp.where(group == w, own, total)
            out.append(total)
    return out


def scatter_fine(site, field, out_ref):
    rows = row_order(True).astype(F32)
    rows = jnp.concatenate([rows, rows, rows], axis=1).astype(BF16)
    lanes = y_order(128, 16, True)
    group = site.lane >> 4
    for p in range(2):
        for c in range(3):
            parts = [x.astype(F32) for x in three_parts(field[3 * p + c])]
            tall = jnp.concatenate([jnp.where(group == w, x, 0.0) for x in parts for w in range(8)], axis=0)
            value = dot(rows, dot(tall.astype(BF16), lanes).astype(BF16))
            for t in range(4):
                for z in range(4):
                    out_ref[p, c, t, z] = value[16 * t + 4 * z : 16 * t + 4 * z + 4]


def kernel_links(links_ref, g_ref, gx_ref):
    prepare_links(Site(), links_ref, g_ref, gx_ref)


def kernel_first(g_ref, block_ref, source_ref, rhs_ref, *outs):
    site = Site()
    rhs = gather_fine(site, source_ref)
    store(rhs_ref, rhs)
    finish_fine(site, g_ref, fine_matrix(site, block_ref, rhs), *outs)


def kernel_smooth(links_ref, block_ref, rhs_ref, *refs):
    site = Site()
    solution, applied = begin_fine(site, links_ref, refs[:8])
    residual = sub(load(rhs_ref, 6), applied)
    solution = add(solution, fine_matrix(site, block_ref, residual))
    finish_fine(site, links_ref, solution, *refs[8:])


def kernel_last(links_ref, rhs_ref, *refs):
    site = Site()
    _, applied = begin_fine(site, links_ref, refs[:8])
    scatter_fine(site, sub(load(rhs_ref, 6), applied), refs[8])


def kernel_own(links_ref, field_ref, acc_ref):
    store(acc_ref, fine_own(Site(), links_ref, load(field_ref, 6)))


def kernel_scatter(field_ref, out_ref):
    scatter_fine(Site(), load(field_ref, 6), out_ref)


def kernel_restrict(links_ref, near_ref, jacobi_ref, rhs_ref, *refs):
    site = Site()
    _, applied = begin_fine(site, links_ref, refs[:8])
    residual = sub(load(rhs_ref, 6), applied)
    mid_res = restrict_fine(site, near_ref, residual)
    store(refs[8], mid_res)
    store(refs[9], mid_matrix(site, jacobi_ref, mid_res))


def neighbours(refs, get):
    nx, t1, z0, z1, t0 = refs
    ahead_t, behind_t = by_parity("ta", get(t0), get(t1))
    ahead_z, behind_z = by_parity("gz", get(z0), get(z1))
    return [ahead_t, ahead_z, get(nx)], [behind_t, behind_z, get(nx)]


def kernel_mid_own(stencil_ref, v_ref, out_ref):
    site = Site()
    store(out_ref, mid_stencil_own(site, stencil_ref, load(v_ref, 3)))


def mid_rest(site, stencil_ref, res_ref, y2_ref, own_ref, around):
    ahead, behind = neighbours(around, lambda r: load(r, 3))
    applied = mid_stencil_near(site, stencil_ref, load(y2_ref, 3), ahead, behind)
    return sub(load(res_ref, 3), add(load(own_ref, 3), applied))


def kernel_mid_down(stencil_ref, near_ref, jacobi_ref, res_ref, y2_ref, own_ref, *refs):
    site = Site()
    around, (r3_ref, y3_ref, tile_ref) = refs[:-3], refs[-3:]
    rest = mid_rest(site, stencil_ref, res_ref, y2_ref, own_ref, around)
    r3 = restrict_mid(site, near_ref, rest, tile_ref)
    r3_ref[...] = r3
    y3_ref[...] = coarse_matrix([(jacobi_ref, 0, r3)])


def kernel_sweep_own(stencil_ref, r3_ref, y3_ref, out_ref):
    out_ref[...] = r3_ref[...] - coarse_stencil_own(stencil_ref, y3_ref[...])


def sweep(stencil_ref, jacobi_ref, own_ref, y3_ref, around):
    ahead, behind = neighbours(around, lambda r: [r[...]])
    ahead, behind = [x[0] for x in ahead], [x[0] for x in behind]
    rest = own_ref[...] - coarse_stencil_near(stencil_ref, ahead, behind)
    return y3_ref[...] + coarse_matrix([(jacobi_ref, 0, rest)])


def kernel_sweep(stencil_ref, jacobi_ref, own_ref, y3_ref, *refs):
    refs[-1][...] = sweep(stencil_ref, jacobi_ref, own_ref, y3_ref, refs[:-1])


def kernel_sweep_up(stencil_ref, jacobi_ref, near_ref, y2_ref, own_ref, y3_ref, *refs):
    site = Site()
    around, (out_ref, row_ref) = refs[:-2], refs[-2:]
    y3 = sweep(stencil_ref, jacobi_ref, own_ref, y3_ref, around)
    store(out_ref, add(load(y2_ref, 3), prolong_mid(site, near_ref, y3, row_ref)))


def kernel_mid_up(links_ref, stencil_ref, jacobi_ref, near_ref, old_ref, res_ref, y2_ref, own_ref, *refs):
    site = Site()
    around, outs, spread_ref = refs[:-6], refs[-6:-1], refs[-1]
    rest = mid_rest(site, stencil_ref, res_ref, y2_ref, own_ref, around)
    y2 = add(load(y2_ref, 3), mid_matrix(site, jacobi_ref, rest))
    solution = add(load(old_ref, 6), prolong_fine(site, near_ref, y2, spread_ref))
    finish_fine(site, links_ref, solution, *outs)


def call(kernel, outs, scratch, *args, after=()):
    def body(*refs):
        kernel(*refs[len(after) :])

    specs = [pl.BlockSpec(memory_space=pl.ANY)] * len(after)
    return pl.pallas_call(
        body,
        out_shape=[jax.ShapeDtypeStruct(*s) if s[1] == BF16 else jax.ShapeDtypeStruct(s, F32) for s in outs],
        in_specs=specs + [pl.BlockSpec(memory_space=pltpu.VMEM)] * len(args),
        scratch_shapes=[pltpu.VMEM(s, F32) for s in scratch],
        compiler_params=pltpu.CompilerParams(vmem_limit_bytes=VMEM_BYTES),
        name=kernel.__name__,
    )(*after, *args)


def from_behind(block, axis, distance):
    n = lax.axis_size(axis)
    return lax.ppermute(block, axis, [((i - distance) % n, i) for i in range(n)])


def swap(block, axis, phase):
    n = lax.axis_size(axis)
    return lax.ppermute(block, axis, [(i, (((i + phase) ^ 1) - phase) % n) for i in range(n)])


def exchange(v):
    x = from_behind(v, "xy", 1)
    t1 = swap(v, "ta", 1)
    z0 = swap(v, "gz", 0)
    z1 = swap(v, "gz", 1)
    t0 = swap(v, "ta", 0)
    return [x, t1, z0, z1, t0]


def exchange_fine(g, gx, sol, z0, z1, t0, t1):
    x = from_behind(sol, "xy", 1)
    t1 = swap(t1, "ta", 1)
    z0 = swap(z0, "gz", 0)
    z1 = swap(z1, "gz", 1)
    t0 = swap(t0, "ta", 0)
    (acc,) = call(kernel_own, [TILE6], [], g, sol)
    return [sol, acc, t0, x, z1, z0, t1, gx]


TILE6 = (6, 8, 128)
FINE_OUT = [TILE6] * 5


def local(
    right_side,
    links,
    block_inverse,
    near_fine,
    mid_stencil,
    mid_jacobi,
    near_mid,
    coarse_stencil,
    coarse_jacobi,
):
    block = block_inverse.reshape(384, 768)
    near1 = near_fine.reshape(192, 768)
    stencil2 = mid_stencil.reshape(1728, 384)
    jacobi2 = mid_jacobi.reshape(192, 384)
    near2 = near_mid.reshape(near_mid.shape[0], near_mid.shape[4])
    stencil3 = jnp.swapaxes(coarse_stencil, 5, 6).reshape(864, 192)
    jacobi3 = jnp.swapaxes(coarse_jacobi, 4, 5).reshape(96, 192)
    mid = (3, 8, 128)
    coarse = (8, 48)

    g, gx = call(kernel_links, [(144, 8, 128), ((18, 16, 128), BF16)], [], links, after=(block,))
    gx = from_behind(gx, "xy", 1)
    rhs, *state = call(kernel_first, [TILE6] + FINE_OUT, [], g, block, right_side)
    for cycle_no in range(CYCLES):
        around = exchange_fine(g, gx, *state)
        r2, y2 = call(kernel_restrict, [mid, mid], [], g, near1, jacobi2, rhs, *around, after=(stencil2,))
        around = exchange(y2)
        (own,) = call(kernel_mid_own, [mid], [], stencil2, y2)
        r3, y3 = call(
            kernel_mid_down, [coarse, coarse], [(2, 48, 128)], stencil2, near2, jacobi3, r2, y2, own, *around
        )
        for _ in range(SWEEPS - 1):
            around = exchange(y3)
            (own,) = call(kernel_sweep_own, [coarse], [], stencil3, r3, y3)
            (y3,) = call(kernel_sweep, [coarse], [], stencil3, jacobi3, own, y3, *around)
        around = exchange(y3)
        (own,) = call(kernel_sweep_own, [coarse], [], stencil3, r3, y3)
        (y2,) = call(
            kernel_sweep_up, [mid], [(2, 48, 128)], stencil3, jacobi3, near2, y2, own, y3, *around
        )
        around = exchange(y2)
        (own,) = call(kernel_mid_own, [mid], [], stencil2, y2)
        state = call(
            kernel_mid_up,
            FINE_OUT,
            [(48, 8, 128)],
            g,
            stencil2,
            jacobi2,
            near1,
            state[0],
            r2,
            y2,
            own,
            *around,
        )
        state = call(kernel_smooth, FINE_OUT, [], g, block, rhs, *exchange_fine(g, gx, *state))
        if cycle_no < CYCLES - 1:
            state = call(kernel_smooth, FINE_OUT, [], g, block, rhs, *exchange_fine(g, gx, *state))
    around = exchange_fine(g, gx, *state)
    (solution,) = call(kernel_scatter, [right_side.shape], [], state[0])
    (residual,) = call(kernel_last, [right_side.shape], [], g, rhs, *around)
    return solution, residual


def solution(mesh):
    return jax.shard_map(
        local,
        mesh=mesh,
        in_specs=(
            P(None, None, "ta", "gz", "xy", None),
            P(None, None, "ta", "gz", "xy", None),
            P(None, "ta", "gz", "xy", None),
            P(None, "ta", "gz", "xy", None),
            P(None, None, "ta", "gz", "xy", None),
            P(None, "ta", "gz", "xy", None),
            P(None, "ta", "gz", "xy", None),
            P(None, None, "ta", "gz", "xy", None, None),
            P(None, "ta", "gz", "xy", None, None),
        ),
        out_specs=(P(None, None, "ta", "gz", "xy", None), P(None, None, "ta", "gz", "xy", None)),
        check_vma=False,
    )
```
